32 devices in a mesh: rep: 2 (over y), fast: 16 (over z, x, core).
Axes of the slice: x: 2, y: 2, z: 4, core: 2. Of those that a mesh axis runs over, the one named last changes fastest.
Arguments:
- tokens: bfloat16 [2, 128, 7168], P(None, ('rep', 'fast')), parts along dimension 1, may hold values from -6 to 6
- expert_ids: int32 [2, 128, 3], P(None, ('rep', 'fast')), parts along dimension 1, may hold values from 0 to 7, all different within a row; in each aligned block of 4 rows (0 to 3, 4 to 7, ..., all dimensions but the last counted through in order) at most 2 rows name the same one
- gate_weights: bfloat16 [2, 128, 3], P(None, ('rep', 'fast')), parts along dimension 1, may hold values from 0.19921875 to 1
- w_gate_up: bfloat16 [7168, 2, 16384], P(None, None, 'fast'), may hold values from -0.0625 to 0.0625
- w_down: bfloat16 [16384, 7168], P('fast'), may hold values from -0.125 to 0.125
- shared_gate_up: bfloat16 [7168, 2, 16384], P(None, None, 'fast'), as said below
- shared_down: bfloat16 [16384, 7168], P('fast'), as said below
Outputs:
- mixed: bfloat16 [2, 128, 7168], P(None, ('rep', 'fast')), parts along dimension 1
The draws below stay inside these ranges and needn't reach their ends.
There are 2 independent parts, one for each index of `rep`. The reference program is written for one: setup_inputs(seed, part) draws one part's arguments, and reference() takes and returns one part's arrays. A program takes and returns all parts, laid end to end along the dimension named above; an argument that names none is the same for every part. Nothing has to cross between parts.
Inputs may be any that keep to these rules, and one draw needn't show every extreme that they name: `expert_ids`: the 3 ids of a token differ. Of the 4 tokens that one device holds in one decode step (an aligned block of rows), at most 2 name one expert, and in every draw some expert is named by exactly 2 of them. `shared_gate_up`: the 8 blocks of 2048 columns are equal copies of one shared expert. `shared_down`: the 8 blocks of 2048 rows are equal copies of one shared expert.
All inputs are finite; a program needn't handle non-finite values.
Results may differ from the reference program's by a relative error of at most 0.0058.
Values may be sent and summed in bfloat16 or wider, within the bound.
No kernel may reach another device: no remote copies, remote signals or barrier semaphores. Data moves between devices by JAX's collectives and lax.ppermute only.
A program may use at most 192 MiB of HBM per device.

```python
import math
import jax
import jax.numpy as jnp
import numpy as np
from jax import lax

D = 7168
FF = 2048
EXPERTS = 8
TOPK = 3
STEPS = 2
TOK_STEP = 4
CAP = 2
TOKENS = 64
N_FAST = 16


def draw_shared_gate_up(key, part):
    base = jnp.clip(jax.random.normal(key, (D, 2, FF), jnp.float32), -6.0, 6.0)
    base = base * D ** (-0.5)
    return jnp.tile(base, (1, 1, EXPERTS)).astype(jnp.bfloat16)


def draw_shared_down(key, part):
    base = jnp.clip(jax.random.normal(key, (FF, D), jnp.float32), -6.0, 6.0)
    base = base * FF ** (-0.5)
    return jnp.tile(base, (EXPERTS, 1)).astype(jnp.bfloat16)


def block_scale(rng, extent, split, least, largest):
    level = 1.0
    for dim, parts in split:
        steps = jax.random.uniform(jax.random.fold_in(jax.random.fold_in(rng, 6), dim), (parts,), jnp.float32, least / len(split), largest / len(split))
        level = level * jnp.repeat(jnp.exp(steps), extent[dim] // parts).reshape((-1,) + (1,) * (len(extent) - 1 - dim))
    return level


def routed_block(rng, own, number, rows, number_of, top, reach, slope):
    ranking = jax.random.permutation(rng, number_of)
    heavy_load, usual = shares(number_of, rows * top, reach, slope, True), shares(number_of, rows * top, reach, slope, False)
    places = jnp.arange(number_of)

    def named(sizes, offset_by):
        used = int((sizes > 0).sum())
        fixed = max(1, used // 4)
        shifted = fixed + (places - fixed + offset_by * (used - fixed)) % max(1, number_of - fixed)
        return jnp.zeros((number_of,), jnp.int32).at[ranking[jnp.where(places < fixed, places, shifted)]].set(jnp.asarray(sizes, jnp.int32))

    sizes = jnp.where(number % 4 == 0, named(heavy_load, number // 4), named(usual, number - number // 4 - 1))
    mixed = jax.random.permutation(jax.random.fold_in(own, 3), number_of)
    donor, receiver = mixed[0:number_of // 2 * 2:2], mixed[1:number_of // 2 * 2:2]
    room = jnp.minimum(sizes[donor] - 1, reach - sizes[receiver]) // 2
    room = jnp.where((donor == ranking[0]) | (receiver == ranking[0]) | (sizes[receiver] == 0), 0, jnp.maximum(room, 0))
    shifted = jax.random.randint(jax.random.fold_in(own, 4), (number_of // 2,), 0, 1 << 20) % (room + 1)
    sizes = sizes.at[donor].add(-shifted).at[receiver].add(shifted)
    members = jnp.searchsorted(jnp.cumsum(sizes), jnp.arange(rows * top), side="right").astype(jnp.int32)
    grid = members.reshape(top, rows).T
    grid = grid[jax.random.permutation(jax.random.fold_in(own, 1), rows)]
    offset_by = jax.random.randint(jax.random.fold_in(own, 2), (rows, 1), 0, top)
    return jnp.take_along_axis(grid, (jnp.arange(top)[None, :] + offset_by) % top, axis=1)


def shares(amount, total, most, skew, full):
    portions = [(1 << 20) // math.isqrt(grade ** skew) + 1 for grade in range(1, amount + 1)]
    largest = most if full else min(most, max(-(-total // amount), total * portions[0] // sum(portions)))
    least = 1 if total - largest >= amount - 1 else 0
    given, spare = [largest] + [least] * (amount - 1), total - largest - least * (amount - 1)
    while spare > 0:
        movable = [i for i in range(1, amount) if given[i] < largest] or [i for i in range(1, amount) if given[i] < most]
        mass, budget = sum([portions[i] for i in movable]), spare
        for i in movable:
            addition = min(most - given[i], max(1, budget * portions[i] // mass), spare)
            given[i] = given[i] + addition
            spare = spare - addition
    return np.array(given)


def normal_values(stream_key, dims, scale, most, shards=(), held_as=jnp.bfloat16):
    entries = scale * jax.random.normal(stream_key, dims, jnp.float32)
    if shards:
        entries = entries * block_scale(stream_key, dims, shards, -0.22, 0.18)
    return jnp.clip(entries, -most, most).astype(held_as)


def setup_inputs(seed: int = 0, part: int = 0) -> dict:
    arg_keys = jax.random.split(jax.random.key(seed), 8)
    part_splits = jax.random.split(jax.random.fold_in(arg_keys[7], part), 8)
    tokens = normal_values(part_splits[0], (STEPS, TOKENS, D), 1.0, 6.0, ((1, 16),))
    expert_ids_keys = jax.random.split(jax.random.fold_in(part_splits[1], 1), STEPS * TOKENS // TOK_STEP)
    expert_ids_turns = jax.random.permutation(jax.random.fold_in(part_splits[1], 3), STEPS * TOKENS // TOK_STEP)
    expert_ids = jax.vmap(lambda own, number: routed_block(jax.random.fold_in(part_splits[1], 2), own, number, TOK_STEP, EXPERTS, TOPK, CAP, 2))(expert_ids_keys, expert_ids_turns).reshape((STEPS, TOKENS, TOPK))
    gate_weights = jnp.clip(0.19921875 + 0.80078125 * jax.random.uniform(part_splits[2], (STEPS, TOKENS, TOPK), jnp.float32) ** block_scale(part_splits[2], (STEPS, TOKENS, TOPK), ((1, 16),), -0.2, 0.2), 0.19921875, 1.0).astype(jnp.bfloat16)
    w_gate_up = normal_values(arg_keys[3], (D, 2, EXPERTS * FF), D ** -0.5, 0.0625, ((2, 16),))
    w_down = normal_values(arg_keys[4], (EXPERTS * FF, D), FF ** -0.5, 0.125, ((0, 16),))
    shared_gate_up = draw_shared_gate_up(jax.random.fold_in(arg_keys[7], 71), part)
    shared_down = draw_shared_down(jax.random.fold_in(arg_keys[7], 71), part)
    return dict(tokens=tokens, expert_ids=expert_ids, gate_weights=gate_weights, w_gate_up=w_gate_up, w_down=w_down, shared_gate_up=shared_gate_up, shared_down=shared_down)


def reference(tokens, expert_ids, gate_weights, w_gate_up, w_down, shared_gate_up, shared_down):
    group_size = N_FAST // EXPERTS
    slice_size = FF // group_size
    row_total = STEPS * TOKENS
    row_bound = STEPS * N_FAST * CAP
    flat_tokens = jnp.concatenate([tokens.reshape(row_total, D), jnp.zeros((1, D), tokens.dtype)], axis=0)
    flat_ids = expert_ids.reshape(row_total, TOPK)
    flat_gates = gate_weights.reshape(row_total, TOPK).astype(jnp.float32)
    shared_up = shared_gate_up[:, :, :FF].reshape(D, 2 * FF)
    shared_out = shared_down[:FF]
    zero_one = jnp.zeros((1,), jnp.float32)

    def per_expert(accum_rows, expert):
        expert_hit = flat_ids == expert
        chosen = jnp.nonzero(jnp.any(expert_hit, axis=1), size=row_bound, fill_value=row_total)[0].astype(jnp.int32)
        gate_row = jnp.concatenate([jnp.sum(jnp.where(expert_hit, flat_gates, 0.0), axis=1), zero_one])[chosen]
        share_row = jnp.concatenate([expert_hit[:, 0].astype(jnp.float32), zero_one])[chosen]
        picked = flat_tokens[chosen]
        routed_up = lax.dynamic_slice_in_dim(w_gate_up, (expert * FF).astype(jnp.int32), FF, 2).reshape(D, 2 * FF)
        routed_down = lax.dynamic_slice_in_dim(w_down, (expert * FF).astype(jnp.int32), FF, 0)
        routed = jnp.dot(picked, routed_up, preferred_element_type=jnp.float32)
        routed_hidden = (jax.nn.silu(routed[:, :FF]) * routed[:, FF:]).astype(jnp.bfloat16)
        common = jnp.dot(picked, shared_up, preferred_element_type=jnp.float32)
        common_hidden = (jax.nn.silu(common[:, :FF]) * common[:, FF:]).astype(jnp.bfloat16)

        def per_slice(running, slice_index):
            first_unit = (slice_index * slice_size).astype(jnp.int32)
            routed_part = jnp.dot(lax.dynamic_slice_in_dim(routed_hidden, first_unit, slice_size, 1),
                                  lax.dynamic_slice_in_dim(routed_down, first_unit, slice_size, 0),
                                  preferred_element_type=jnp.float32)
            shared_part = jnp.dot(lax.dynamic_slice_in_dim(common_hidden, first_unit, slice_size, 1),
                                  lax.dynamic_slice_in_dim(shared_out, first_unit, slice_size, 0),
                                  preferred_element_type=jnp.float32)
            slice_part = (gate_row[:, None] * routed_part + share_row[:, None] * shared_part).astype(jnp.bfloat16)
            return running + slice_part.astype(jnp.float32), None

        expert_sum, _ = lax.scan(per_slice, jnp.zeros((row_bound, D), jnp.float32),
                                 jnp.arange(group_size, dtype=jnp.int32))
        return accum_rows.at[chosen].add(expert_sum), None

    accum_rows, _ = lax.scan(per_expert, jnp.zeros((row_total + 1, D), jnp.float32),
                             jnp.arange(EXPERTS, dtype=jnp.int32))
    return accum_rows[:row_total].reshape(STEPS, TOKENS, D).astype(jnp.bfloat16)
```

```python
import functools
import math

import jax
import jax.numpy as jnp
from jax import lax
from jax.experimental import pallas as pl
from jax.experimental.pallas import tpu as pltpu
from jax.sharding import PartitionSpec as P

EXPERTS = 8
TOPK = 3
STEPS = 2
CAP = 2
VMEM_GRANT = 8 * 2**20
DOWN_PIECES = 7


def slot_tables(step_tokens, step_ids, step_gates):
    tok_count = step_ids.shape[0]
    flat_ids = step_ids.reshape(tok_count * TOPK)
    expert_hit = (flat_ids[:, None] == jnp.arange(EXPERTS, dtype=jnp.int32)[None, :]).astype(
        jnp.int32
    )
    slot_rank = jnp.sum((jnp.cumsum(expert_hit, axis=0) - expert_hit) * expert_hit, axis=1)
    slot_index = flat_ids * CAP + slot_rank
    placed = (slot_index[:, None] == jnp.arange(EXPERTS * CAP, dtype=jnp.int32)[None, :]).astype(
        jnp.float32
    )
    selector = jnp.sum(placed.reshape(tok_count, TOPK, EXPERTS * CAP), axis=1)
    blocks = jnp.einsum(
        "ts,td->sd", selector.astype(jnp.bfloat16), step_tokens, preferred_element_type=jnp.float32
    ).astype(jnp.bfloat16)
    share_row = jnp.broadcast_to(
        (jnp.arange(TOPK) == 0).astype(jnp.float32)[None, :], (tok_count, TOPK)
    ).reshape(-1)
    gate_row = step_gates.astype(jnp.float32).reshape(-1)
    slot_coefs = jnp.einsum(
        "rs,rc->sc",
        placed,
        jnp.stack([gate_row, share_row], axis=1),
        precision=lax.Precision.HIGHEST,
    ).astype(jnp.bfloat16)
    return (blocks.reshape(EXPERTS, CAP, -1), slot_coefs.reshape(EXPERTS, CAP, 2), selector)


def send_out(blocks, slot_coefs, group_size):
    spread = jnp.repeat(blocks, group_size, axis=0)
    spread_coefs = jnp.repeat(slot_coefs, group_size, axis=0)
    arrived, arrived_coefs = (
        lax.all_to_all(spread, "fast", split_axis=0, concat_axis=0, tiled=True),
        lax.all_to_all(spread_coefs, "fast", split_axis=0, concat_axis=0, tiled=True),
    )
    return (arrived, arrived_coefs)


def expert_work(arrived, arrived_coefs, weights):
    w_gate_up, w_down, shared_gate_up, shared_down = weights
    model_width = arrived.shape[-1]
    hidden_size = w_down.shape[0]
    flat_rows = arrived.reshape(-1, model_width)
    flat_coef = arrived_coefs.reshape(-1, 2).astype(jnp.float32)
    row_count = flat_rows.shape[0]
    block_rows = math.gcd(row_count, 512)
    routed_up = w_gate_up.reshape(model_width, 2 * hidden_size)
    common_up = shared_gate_up.reshape(model_width, 2 * hidden_size)

    def one_block(block_pair):
        row_block, slot_coef = block_pair
        routed = jnp.dot(row_block, routed_up, preferred_element_type=jnp.float32)
        routed_hidden = (jax.nn.silu(routed[:, :hidden_size]) * routed[:, hidden_size:]).astype(
            jnp.bfloat16
        )
        common = jnp.dot(row_block, common_up, preferred_element_type=jnp.float32)
        common_hidden = (jax.nn.silu(common[:, :hidden_size]) * common[:, hidden_size:]).astype(
            jnp.bfloat16
        )
        result = slot_coef[:, 0:1] * jnp.dot(
            routed_hidden, w_down, preferred_element_type=jnp.float32
        )
        result = result + slot_coef[:, 1:2] * jnp.dot(
            common_hidden, shared_down, preferred_element_type=jnp.float32
        )
        return result.astype(jnp.bfloat16)

    outcome = lax.map(
        one_block,
        (flat_rows.reshape(-1, block_rows, model_width), flat_coef.reshape(-1, block_rows, 2)),
    )
    return outcome.reshape(arrived.shape)


def round_trip(blocks, slot_coefs, weights, group_size):
    arrived, arrived_coefs = send_out(blocks, slot_coefs, group_size)
    partials = expert_work(arrived, arrived_coefs, weights)
    returned = lax.all_to_all(partials, "fast", split_axis=0, concat_axis=0, tiled=True)
    slot_count = blocks.shape[1]
    return returned.reshape(EXPERTS, group_size, slot_count, -1).astype(jnp.float32).sum(axis=1)


def finish(selector, summed):
    flat_sums = summed.reshape(selector.shape[1], -1)
    return jnp.dot(
        selector, flat_sums, precision=lax.Precision.HIGHEST, preferred_element_type=jnp.float32
    ).astype(jnp.bfloat16)


def local(tokens, expert_ids, gate_weights, w_gate_up, w_down, shared_gate_up, shared_down):
    group_size = lax.axis_size("fast") // EXPERTS
    if group_size == 2 and w_down.shape[0] % 256 == 0 and tokens.shape[-1] % (DOWN_PIECES * 1024) == 0:
        return by_chip(
            tokens, expert_ids, gate_weights, w_gate_up, w_down, shared_gate_up, shared_down
        )
    weights = (w_gate_up, w_down, shared_gate_up, shared_down)
    prepared = [
        slot_tables(tokens[step_index], expert_ids[step_index], gate_weights[step_index])
        for step_index in range(STEPS)
    ]
    outputs = []
    model_width = tokens.shape[-1]
    blocks = jnp.stack([member[0] for member in prepared], axis=1).reshape(
        EXPERTS, STEPS * CAP, model_width
    )
    slot_coefs = jnp.stack([member[1] for member in prepared], axis=1).reshape(
        EXPERTS, STEPS * CAP, 2
    )
    summed = round_trip(blocks, slot_coefs, weights, group_size).reshape(
        EXPERTS, STEPS, CAP, model_width
    )
    for step_index in range(STEPS):
        outputs.append(finish(prepared[step_index][2], summed[:, step_index]))
    return jnp.stack(outputs, axis=0)


def vm_params(flops=0, moved=0):
    return dict(
        compiler_params=pltpu.CompilerParams(vmem_limit_bytes=VMEM_GRANT),
        cost_estimate=pl.CostEstimate(flops=flops, bytes_accessed=moved, transcendentals=0),
    )


def in_vmem():
    return pl.BlockSpec(memory_space=pltpu.VMEM)


def in_smem():
    return pl.BlockSpec(memory_space=pltpu.SMEM)


def anywhere():
    return pl.BlockSpec(memory_space=pltpu.HBM)


def core_side():
    return lax.rem(lax.axis_index("fast"), 2)


def slot_numbers(ids_ref):
    choices, steps, tok_count = ids_ref.shape
    numbers = {}
    for s in range(steps):
        ids = [[ids_ref[k, s, t] for k in range(choices)] for t in range(tok_count)]
        for t in range(tok_count):
            for k in range(choices):
                rank = jnp.int32(0)
                for earlier in range(t):
                    for other in ids[earlier]:
                        rank = rank + (other == ids[t][k]).astype(jnp.int32)
                numbers[s, t, k] = ids[t][k] * (steps * CAP) + s * CAP + rank
    return numbers


def stacked_tokens(tok_ref):
    parts = [tok_ref[s].astype(jnp.float32) for s in range(tok_ref.shape[0])]
    return jnp.concatenate(parts, axis=0).astype(jnp.bfloat16)


def pack_kernel(ids_ref, tok_ref, send_ref, flat_ref):
    steps, tok_count, width = tok_ref.shape
    rows, slots = steps * tok_count, EXPERTS * steps * CAP
    half = width // 2
    numbers = slot_numbers(ids_ref)
    place = lax.broadcasted_iota(jnp.int32, (slots, rows), 0) * rows + lax.broadcasted_iota(
        jnp.int32, (slots, rows), 1
    )
    selector = jnp.zeros((slots, rows), jnp.float32)
    for (s, t, k), number in numbers.items():
        selector = jnp.where(place == number * rows + (s * tok_count + t), 1.0, selector)
    flat = stacked_tokens(tok_ref)
    flat_ref[...] = flat
    blocks = jnp.dot(selector.astype(jnp.bfloat16), flat, preferred_element_type=jnp.float32)
    per = steps * CAP
    for e in range(EXPERTS):
        for g in range(2):
            piece = blocks[e * per : (e + 1) * per, g * half : (g + 1) * half]
            send_ref[2 * e + g] = piece.astype(jnp.bfloat16)


def pack_tokens(tokens, expert_ids):
    steps, tok_count, width = tokens.shape
    return pl.pallas_call(
        pack_kernel,
        out_shape=(
            jax.ShapeDtypeStruct((2 * EXPERTS, steps * CAP, width // 2), jnp.bfloat16),
            jax.ShapeDtypeStruct((steps * tok_count, width), jnp.bfloat16),
        ),
        in_specs=[in_smem(), in_vmem()],
        out_specs=(in_vmem(), in_vmem()),
        name="pack_tokens",
        **vm_params(10**6, 10**6),
    )(expert_ids, tokens)


def up_copies(up_ref, held_ref, sems, first):
    depth = held_ref.shape[1]
    return [
        pltpu.make_async_copy(
            up_ref.at[pl.ds(first, depth), :, pl.ds(c * 128, 128)], held_ref.at[c], sems.at[c]
        )
        for c in range(held_ref.shape[0])
    ]


def rows_in_turn(held):
    return held.reshape(held.shape[0], -1, 128)


def spread_matrix():
    row = lax.broadcasted_iota(jnp.int32, (128, 512), 0)
    col = lax.broadcasted_iota(jnp.int32, (128, 512), 1)
    target = jnp.where(col < 256, 2 * row, 2 * row + 257)
    return jnp.where(col == target, 1.0, 0.0).astype(jnp.bfloat16)


def spread_rows(x_ref, spread_ref, batch):
    rows, width = x_ref.shape
    matrix = spread_matrix()

    def step(i, carry):
        at = pl.multiple_of(i * 128 * batch, 128 * batch)
        chunk = jnp.concatenate(
            [x_ref[:, pl.ds(at + 128 * b, 128)] for b in range(batch)], axis=0
        )
        wide = jnp.dot(chunk, matrix, preferred_element_type=jnp.float32).astype(jnp.bfloat16)
        to = pl.multiple_of(i * 256 * batch, 256 * batch)
        for b in range(batch):
            piece = wide[b * rows : (b + 1) * rows]
            spread_ref[0:rows, pl.ds(to + 256 * b, 256)] = piece[:, :256]
            spread_ref[rows : 2 * rows, pl.ds(to + 256 * b, 256)] = piece[:, 256:]
        return carry

    lax.fori_loop(0, width // (128 * batch), step, 0)


def up_matmul(spread_ref, up_ref, acc_ref):
    depth = spread_ref.shape[1]
    chunk = depth // 7

    def step(i, carry):
        src = pl.ds(pl.multiple_of(i * chunk, chunk), chunk)
        rows = spread_ref[:, src]
        for p in range(up_ref.shape[0] // 2):
            pair = jnp.concatenate([up_ref[2 * p, src, :], up_ref[2 * p + 1, src, :]], axis=1)
            acc_ref[:, p * 256 : (p + 1) * 256] += jnp.dot(
                rows, pair, preferred_element_type=jnp.float32
            )
        return carry

    lax.fori_loop(0, depth // chunk, step, 0)


def hidden_of(acc_ref):
    rows = acc_ref.shape[0] // 2
    gate, up = acc_ref[0:rows], acc_ref[rows : 2 * rows]
    return (jax.nn.silu(gate) * up).astype(jnp.bfloat16)


def down_matmul(hidden, down_ref, first, out_ref, chunk):
    def step(i, carry):
        at = pl.multiple_of(i * chunk, chunk)
        out_ref[:, pl.ds(at, chunk)] = jnp.dot(
            hidden[...],
            down_ref[:, pl.ds(pl.multiple_of(first + at, chunk), chunk)],
            preferred_element_type=jnp.float32,
        ).astype(out_ref.dtype)
        return carry

    lax.fori_loop(0, out_ref.shape[1] // chunk, step, 0)


def flatten_rows(block_ref, flat_ref):
    sources, per, _ = block_ref.shape
    group = max(1, 16 // per)
    for i in range(0, sources, group):
        rows = jnp.concatenate(
            [block_ref[i + j].astype(jnp.float32) for j in range(group)], axis=0
        )
        flat_ref[i * per : (i + group) * per] = rows.astype(flat_ref.dtype)


def half_fetch_kernel(block_ref, up_ref, held_ref, spread_ref, sems, flat_ref):
    copies = up_copies(up_ref, held_ref, sems, core_side() * held_ref.shape[1])
    for copy in copies:
        copy.start()
    flatten_rows(block_ref, flat_ref)
    spread_rows(flat_ref, spread_ref, 4)
    for copy in copies:
        copy.wait()


def first_up_kernel(ready_ref, spread_ref, block_ref, up_ref, held_ref, next_ref, acc_ref, sems,
                    flat_ref):
    copies = up_copies(up_ref, held_ref, sems, (1 - core_side()) * held_ref.shape[1])
    for copy in copies:
        copy.start()
    flatten_rows(block_ref, flat_ref)
    spread_rows(flat_ref, next_ref, 4)
    acc_ref[...] = jnp.zeros_like(acc_ref)
    up_matmul(spread_ref, ready_ref, acc_ref)
    for copy in copies:
        copy.wait()


def second_up_kernel(ready_ref, spread_ref, part_ref, down_ref, hid_ref, held_ref, out_ref, sems,
                     acc_ref):
    half = out_ref.shape[1]
    chunk = half // DOWN_PIECES
    side = core_side()

    def piece(first, i):
        at = pl.ds(pl.multiple_of(first + i * chunk, chunk), chunk)
        return pltpu.make_async_copy(down_ref.at[:, at], held_ref.at[:, at], sems.at[i])

    theirs = [piece((1 - side) * half, i) for i in range(DOWN_PIECES)]
    mine = pl.ds(pl.multiple_of(side * half, half), half)
    rest = pltpu.make_async_copy(
        down_ref.at[:, mine], held_ref.at[:, mine], sems.at[DOWN_PIECES]
    )
    for copy in theirs:
        copy.start()
    rest.start()
    acc_ref[...] = part_ref[...]
    up_matmul(spread_ref, ready_ref, acc_ref)
    hid_ref[...] = hidden_of(acc_ref)
    for i, copy in enumerate(theirs):
        copy.wait()
        at = pl.ds(pl.multiple_of((1 - side) * half + i * chunk, chunk), chunk)
        out_ref[:, i * chunk : (i + 1) * chunk] = jnp.dot(
            hid_ref[...], held_ref[:, at], preferred_element_type=jnp.float32
        ).astype(out_ref.dtype)
    rest.wait()


def own_down_kernel(hid_ref, down_ref, out_ref):
    down_matmul(hid_ref, down_ref, core_side() * out_ref.shape[1], out_ref, out_ref.shape[1] // 7)


def routed_part(mine, up, down, swap):
    sources, per, half = mine.shape
    rows, hidden = sources * per, down.shape[0]
    tiles = hidden // 128
    held_half = pltpu.VMEM((tiles, half, 2, 128), jnp.bfloat16)
    spread = pltpu.VMEM((2 * rows, 2 * half), jnp.bfloat16)
    sems = pltpu.SemaphoreType.DMA((tiles,))
    flat = pltpu.VMEM((rows, half), jnp.bfloat16)
    theirs = swap(mine)
    held, spread_mine = pl.pallas_call(
        half_fetch_kernel,
        out_shape=(held_half, spread),
        in_specs=[in_vmem(), anywhere()],
        out_specs=(in_vmem(), in_vmem()),
        scratch_shapes=[sems, flat],
        name="half_fetch",
        **vm_params(0, up.size),
    )(mine, up)
    held, spread_theirs, part = pl.pallas_call(
        first_up_kernel,
        out_shape=(
            held_half, spread, pltpu.VMEM((2 * rows, hidden), jnp.float32)
        ),
        in_specs=[in_vmem()] * 3 + [anywhere()],
        out_specs=(in_vmem(),) * 3,
        scratch_shapes=[sems, flat],
        name="first_up",
        **vm_params(8 * rows * half * hidden, up.size),
    )(rows_in_turn(held), spread_mine, theirs, up)
    hid, down_held, sent = pl.pallas_call(
        second_up_kernel,
        out_shape=(
            pltpu.VMEM((rows, hidden), jnp.bfloat16),
            pltpu.VMEM(down.shape, jnp.bfloat16),
            jax.ShapeDtypeStruct((rows, half), jnp.bfloat16),
        ),
        in_specs=[in_vmem()] * 3 + [anywhere()],
        out_specs=(in_vmem(),) * 3,
        scratch_shapes=[
            pltpu.SemaphoreType.DMA((DOWN_PIECES + 1,)),
            pltpu.VMEM((2 * rows, hidden), jnp.float32),
        ],
        name="second_up",
        **vm_params(10 * rows * half * hidden, 2 * down.size),
    )(rows_in_turn(held), spread_theirs, part, down)
    got = swap(sent)
    kept = pl.pallas_call(
        own_down_kernel,
        out_shape=pltpu.VMEM((rows, half), jnp.float32),
        in_specs=[in_vmem()] * 2,
        out_specs=in_vmem(),
        name="own_down",
        **vm_params(2 * rows * half * hidden, 10**7),
    )(hid, down_held)
    return pl.pallas_call(
        add_kernel,
        out_shape=jax.ShapeDtypeStruct(mine.shape, jnp.bfloat16),
        in_specs=[in_vmem()] * 2,
        out_specs=in_vmem(),
        name="add_halves",
        **vm_params(rows * half, 10**6),
    )(kept, got)


def add_kernel(kept_ref, got_ref, out_ref):
    total = kept_ref[...] + got_ref[...].astype(jnp.float32)
    per = out_ref.shape[1]
    for i in range(out_ref.shape[0]):
        out_ref[i] = total[i * per : (i + 1) * per].astype(jnp.bfloat16)


def join_rows(mine_ref, theirs_ref, index, flat_ref):
    rows, depth = flat_ref.shape
    cols = slice(index * depth, (index + 1) * depth)
    flat_ref[0 : rows // 2] = mine_ref[:, cols]
    flat_ref[rows // 2 : rows] = theirs_ref[:, cols]


def shared_fetch_kernel(mine_ref, theirs_ref, up_ref, held_ref, spread_ref, sems, flat_ref):
    copies = up_copies(up_ref, held_ref, sems, 0)
    for copy in copies:
        copy.start()
    join_rows(mine_ref, theirs_ref, 0, flat_ref)
    spread_rows(flat_ref, spread_ref, 14)
    for copy in copies:
        copy.wait()


def shared_first_kernel(ready_ref, spread_ref, mine_ref, theirs_ref, up_ref, held_ref, next_ref,
                        acc_ref, sems, flat_ref):
    copies = up_copies(up_ref, held_ref, sems, held_ref.shape[1])
    for copy in copies:
        copy.start()
    join_rows(mine_ref, theirs_ref, 1, flat_ref)
    spread_rows(flat_ref, next_ref, 14)
    acc_ref[...] = jnp.zeros_like(acc_ref)
    up_matmul(spread_ref, ready_ref, acc_ref)
    for copy in copies:
        copy.wait()


def shared_second_kernel(ready_ref, spread_ref, part_ref, hid_ref, acc_ref):
    acc_ref[...] = part_ref[...]
    up_matmul(spread_ref, ready_ref, acc_ref)
    hid_ref[...] = hidden_of(acc_ref)


def shared_hidden(mine, theirs, up):
    width, _, hidden = up.shape
    rows, tiles, half = 2 * mine.shape[0], hidden // 128, width // 2
    held_half = pltpu.VMEM((tiles, half, 2, 128), jnp.bfloat16)
    spread = pltpu.VMEM((2 * rows, 2 * half), jnp.bfloat16)
    sems = pltpu.SemaphoreType.DMA((tiles,))
    flat = pltpu.VMEM((rows, half), jnp.bfloat16)
    held, spread_now = pl.pallas_call(
        shared_fetch_kernel,
        out_shape=(held_half, spread),
        in_specs=[in_vmem(), in_vmem(), anywhere()],
        out_specs=(in_vmem(), in_vmem()),
        scratch_shapes=[sems, flat],
        name="shared_fetch",
        **vm_params(0, up.size),
    )(mine, theirs, up)
    held, spread_now, part = pl.pallas_call(
        shared_first_kernel,
        out_shape=(held_half, spread, pltpu.VMEM((2 * rows, hidden), jnp.float32)),
        in_specs=[in_vmem()] * 4 + [anywhere()],
        out_specs=(in_vmem(),) * 3,
        scratch_shapes=[sems, flat],
        name="shared_first",
        **vm_params(0, up.size),
    )(rows_in_turn(held), spread_now, mine, theirs, up)
    return pl.pallas_call(
        shared_second_kernel,
        out_shape=jax.ShapeDtypeStruct((rows, hidden), jnp.bfloat16),
        in_specs=[in_vmem()] * 3,
        out_specs=in_vmem(),
        scratch_shapes=[pltpu.VMEM((2 * rows, hidden), jnp.float32)],
        name="shared_second",
        **vm_params(0, up.size // 2),
    )(rows_in_turn(held), spread_now, part)


def shared_down_kernel(hid_ref, down_ref, mine_ref, theirs_ref, held_ref, sems):
    count, _, chunk = held_ref.shape
    rows = mine_ref.shape[0]

    def piece(i):
        return pltpu.make_async_copy(
            down_ref.at[:, pl.ds(i * chunk, chunk)], held_ref.at[i], sems.at[i]
        )

    copies = [piece(i) for i in range(count)]
    for copy in copies:
        copy.start()
    for i, copy in enumerate(copies):
        copy.wait()
        part = jnp.dot(hid_ref[...], held_ref[i], preferred_element_type=jnp.float32)
        cols = slice(i * chunk, (i + 1) * chunk)
        mine_ref[:, cols] = part[0:rows]
        theirs_ref[:, cols] = part[rows : 2 * rows].astype(jnp.bfloat16)


def shared_out(hid, down):
    rows, (hidden, width) = hid.shape[0] // 2, down.shape
    chunk = width // (2 * DOWN_PIECES)
    return pl.pallas_call(
        shared_down_kernel,
        out_shape=(
            jax.ShapeDtypeStruct((rows, width), jnp.float32),
            jax.ShapeDtypeStruct((rows, width), jnp.bfloat16),
        ),
        in_specs=[in_vmem(), anywhere()],
        out_specs=(in_vmem(), in_vmem()),
        scratch_shapes=[
            pltpu.VMEM((2 * DOWN_PIECES, hidden, chunk), jnp.bfloat16),
            pltpu.SemaphoreType.DMA((2 * DOWN_PIECES,)),
        ],
        name="shared_down",
        compiler_params=pltpu.CompilerParams(vmem_limit_bytes=3 * VMEM_GRANT),
        cost_estimate=pl.CostEstimate(
            flops=0, bytes_accessed=2 * down.size, transcendentals=0
        ),
    )(hid, down)


def combine_kernel(ids_ref, gates_ref, back_ref, kept_ref, got_ref, out_ref):
    steps, tok_count, width = out_ref.shape
    rows, per = steps * tok_count, back_ref.shape[1]
    slots = EXPERTS * per
    half = width // 2
    numbers = slot_numbers(ids_ref)
    place = lax.broadcasted_iota(jnp.int32, (rows, slots), 0) * slots + lax.broadcasted_iota(
        jnp.int32, (rows, slots), 1
    )
    weights = jnp.zeros((rows, slots), jnp.float32)
    for (s, t, k), number in numbers.items():
        weights = jnp.where(
            place == (s * tok_count + t) * slots + number, gates_ref[k, s, t], weights
        )
    weights = weights.astype(jnp.bfloat16)
    for g in range(2):
        parts = jnp.concatenate(
            [back_ref[2 * e + g].astype(jnp.float32) for e in range(EXPERTS)], axis=0
        ).astype(jnp.bfloat16)
        total = jnp.dot(weights, parts, preferred_element_type=jnp.float32)
        cols = slice(g * half, (g + 1) * half)
        total = total + (kept_ref[:, cols] + got_ref[:, cols].astype(jnp.float32))
        for s in range(steps):
            out_ref[s, :, cols] = total[
                s * tok_count : (s + 1) * tok_count
            ].astype(jnp.bfloat16)


def combine(expert_ids, gates, back, kept, got, like):
    return pl.pallas_call(
        combine_kernel,
        out_shape=jax.ShapeDtypeStruct(like.shape, jnp.bfloat16),
        in_specs=[in_smem(), in_smem()] + [in_vmem()] * 3,
        out_specs=in_vmem(),
        name="combine",
        **vm_params(10**6, 10**6),
    )(expert_ids, gates, back, kept, got)


def by_chip(tokens, expert_ids, gate_weights, w_gate_up, w_down, shared_gate_up, shared_down):
    pairs = [(i, i ^ 1) for i in range(lax.axis_size("fast"))]

    def swap(x):
        return lax.ppermute(x, "fast", pairs)

    def exchange(x):
        return lax.all_to_all(x, "fast", split_axis=0, concat_axis=0, tiled=True)

    gates = jnp.transpose(gate_weights, (2, 0, 1)).astype(jnp.float32)
    expert_ids = jnp.transpose(expert_ids, (2, 0, 1))
    weights = (w_gate_up, w_down, shared_gate_up, shared_down)
    w_gate_up, w_down, shared_gate_up, shared_down = (
        pltpu.with_memory_space_constraint(w, pltpu.HBM) for w in weights
    )
    send, flat = pack_tokens(tokens, expert_ids)
    arrived = exchange(send)
    hid = shared_hidden(flat, swap(flat), shared_gate_up)
    arrived, hid = lax.optimization_barrier((arrived, hid))
    partials = routed_part(arrived, w_gate_up, w_down, swap)
    partials, hid = lax.optimization_barrier((partials, hid))
    back = exchange(partials)
    kept, sent = shared_out(hid, shared_down)
    return combine(expert_ids, gates, back, kept, swap(sent), tokens)


def solution(mesh):
    placed = (
        P(None, ("rep", "fast"), None),
        P(None, ("rep", "fast"), None),
        P(None, ("rep", "fast"), None),
        P(None, None, "fast"),
        P("fast", None),
        P(None, None, "fast"),
        P("fast", None),
    )
    return jax.shard_map(
        local, mesh=mesh, in_specs=placed, out_specs=P(None, ("rep", "fast"), None), check_vma=False
    )
```

```python
import functools
import math

import jax
import jax.numpy as jnp
from jax import lax
from jax.experimental import pallas as pl
from jax.experimental.pallas import tpu as pltpu
from jax.sharding import PartitionSpec as P

EXPERTS = 8
TOPK = 3
STEPS = 2
CAP = 2
VMEM_GRANT = 8 * 2**20
DOWN_PIECES = 7
UP_ROWS = 7 * 256


def slot_tables(step_tokens, step_ids, step_gates):
    tok_count = step_ids.shape[0]
    flat_ids = step_ids.reshape(tok_count * TOPK)
    expert_hit = (flat_ids[:, None] == jnp.arange(EXPERTS, dtype=jnp.int32)[None, :]).astype(
        jnp.int32
    )
    slot_rank = jnp.sum((jnp.cumsum(expert_hit, axis=0) - expert_hit) * expert_hit, axis=1)
    slot_index = flat_ids * CAP + slot_rank
    placed = (slot_index[:, None] == jnp.arange(EXPERTS * CAP, dtype=jnp.int32)[None, :]).astype(
        jnp.float32
    )
    selector = jnp.sum(placed.reshape(tok_count, TOPK, EXPERTS * CAP), axis=1)
    blocks = jnp.einsum(
        "ts,td->sd", selector.astype(jnp.bfloat16), step_tokens, preferred_element_type=jnp.float32
    ).astype(jnp.bfloat16)
    share_row = jnp.broadcast_to(
        (jnp.arange(TOPK) == 0).astype(jnp.float32)[None, :], (tok_count, TOPK)
    ).reshape(-1)
    gate_row = step_gates.astype(jnp.float32).reshape(-1)
    slot_coefs = jnp.einsum(
        "rs,rc->sc",
        placed,
        jnp.stack([gate_row, share_row], axis=1),
        precision=lax.Precision.HIGHEST,
    ).astype(jnp.bfloat16)
    return (blocks.reshape(EXPERTS, CAP, -1), slot_coefs.reshape(EXPERTS, CAP, 2), selector)


def send_out(blocks, slot_coefs, group_size):
    spread = jnp.repeat(blocks, group_size, axis=0)
    spread_coefs = jnp.repeat(slot_coefs, group_size, axis=0)
    arrived, arrived_coefs = (
        lax.all_to_all(spread, "fast", split_axis=0, concat_axis=0, tiled=True),
        lax.all_to_all(spread_coefs, "fast", split_axis=0, concat_axis=0, tiled=True),
    )
    return (arrived, arrived_coefs)


def expert_work(arrived, arrived_coefs, weights):
    w_gate_up, w_down, shared_gate_up, shared_down = weights
    model_width = arrived.shape[-1]
    hidden_size = w_down.shape[0]
    flat_rows = arrived.reshape(-1, model_width)
    flat_coef = arrived_coefs.reshape(-1, 2).astype(jnp.float32)
    row_count = flat_rows.shape[0]
    block_rows = math.gcd(row_count, 512)
    routed_up = w_gate_up.reshape(model_width, 2 * hidden_size)
    common_up = shared_gate_up.reshape(model_width, 2 * hidden_size)

    def one_block(block_pair):
        row_block, slot_coef = block_pair
        routed = jnp.dot(row_block, routed_up, preferred_element_type=jnp.float32)
        routed_hidden = (jax.nn.silu(routed[:, :hidden_size]) * routed[:, hidden_size:]).astype(
            jnp.bfloat16
        )
        common = jnp.dot(row_block, common_up, preferred_element_type=jnp.float32)
        common_hidden = (jax.nn.silu(common[:, :hidden_size]) * common[:, hidden_size:]).astype(
            jnp.bfloat16
        )
        result = slot_coef[:, 0:1] * jnp.dot(
            routed_hidden, w_down, preferred_element_type=jnp.float32
        )
        result = result + slot_coef[:, 1:2] * jnp.dot(
            common_hidden, shared_down, preferred_element_type=jnp.float32
        )
        return result.astype(jnp.bfloat16)

    outcome = lax.map(
        one_block,
        (flat_rows.reshape(-1, block_rows, model_width), flat_coef.reshape(-1, block_rows, 2)),
    )
    return outcome.reshape(arrived.shape)


def round_trip(blocks, slot_coefs, weights, group_size):
    arrived, arrived_coefs = send_out(blocks, slot_coefs, group_size)
    partials = expert_work(arrived, arrived_coefs, weights)
    returned = lax.all_to_all(partials, "fast", split_axis=0, concat_axis=0, tiled=True)
    slot_count = blocks.shape[1]
    return returned.reshape(EXPERTS, group_size, slot_count, -1).astype(jnp.float32).sum(axis=1)


def finish(selector, summed):
    flat_sums = summed.reshape(selector.shape[1], -1)
    return jnp.dot(
        selector, flat_sums, precision=lax.Precision.HIGHEST, preferred_element_type=jnp.float32
    ).astype(jnp.bfloat16)


def local(tokens, expert_ids, gate_weights, w_gate_up, w_down, shared_gate_up, shared_down):
    group_size = lax.axis_size("fast") // EXPERTS
    if group_size == 2 and w_down.shape[0] % 256 == 0 and tokens.shape[-1] % (DOWN_PIECES * 1024) == 0:
        return by_chip(
            tokens, expert_ids, gate_weights, w_gate_up, w_down, shared_gate_up, shared_down
        )
    weights = (w_gate_up, w_down, shared_gate_up, shared_down)
    prepared = [
        slot_tables(tokens[step_index], expert_ids[step_index], gate_weights[step_index])
        for step_index in range(STEPS)
    ]
    outputs = []
    model_width = tokens.shape[-1]
    blocks = jnp.stack([member[0] for member in prepared], axis=1).reshape(
        EXPERTS, STEPS * CAP, model_width
    )
    slot_coefs = jnp.stack([member[1] for member in prepared], axis=1).reshape(
        EXPERTS, STEPS * CAP, 2
    )
    summed = round_trip(blocks, slot_coefs, weights, group_size).reshape(
        EXPERTS, STEPS, CAP, model_width
    )
    for step_index in range(STEPS):
        outputs.append(finish(prepared[step_index][2], summed[:, step_index]))
    return jnp.stack(outputs, axis=0)


def vm_params(flops=0, moved=0):
    return dict(
        compiler_params=pltpu.CompilerParams(vmem_limit_bytes=VMEM_GRANT),
        cost_estimate=pl.CostEstimate(flops=flops, bytes_accessed=moved, transcendentals=0),
    )


def in_vmem():
    return pl.BlockSpec(memory_space=pltpu.VMEM)


def in_smem():
    return pl.BlockSpec(memory_space=pltpu.SMEM)


def anywhere():
    return pl.BlockSpec(memory_space=pltpu.HBM)


def in_hbm(x):
    return pltpu.with_memory_space_constraint(x, pltpu.HBM)


def core_side():
    return lax.rem(lax.axis_index("fast"), 2)


def slot_numbers(ids_ref):
    choices, steps, tok_count = ids_ref.shape
    numbers = {}
    for s in range(steps):
        ids = [[ids_ref[k, s, t] for k in range(choices)] for t in range(tok_count)]
        for t in range(tok_count):
            for k in range(choices):
                rank = jnp.int32(0)
                for earlier in range(t):
                    for other in ids[earlier]:
                        rank = rank + (other == ids[t][k]).astype(jnp.int32)
                numbers[s, t, k] = ids[t][k] * (steps * CAP) + s * CAP + rank
    return numbers


def stacked_tokens(tok_ref):
    parts = [tok_ref[s].astype(jnp.float32) for s in range(tok_ref.shape[0])]
    return jnp.concatenate(parts, axis=0).astype(jnp.bfloat16)


def pack_kernel(ids_hbm, tok_hbm, send_ref, flat_ref, ids_ref, tok_ref, sems):
    copies = [
        pltpu.make_async_copy(ids_hbm, ids_ref, sems.at[0]),
        pltpu.make_async_copy(tok_hbm, tok_ref, sems.at[1]),
    ]
    for copy in copies:
        copy.start()
    for copy in copies:
        copy.wait()
    steps, tok_count, width = tok_ref.shape
    rows, slots = steps * tok_count, EXPERTS * steps * CAP
    half = width // 2
    numbers = slot_numbers(ids_ref)
    place = lax.broadcasted_iota(jnp.int32, (slots, rows), 0) * rows + lax.broadcasted_iota(
        jnp.int32, (slots, rows), 1
    )
    selector = jnp.zeros((slots, rows), jnp.float32)
    for (s, t, k), number in numbers.items():
        selector = jnp.where(place == number * rows + (s * tok_count + t), 1.0, selector)
    flat = stacked_tokens(tok_ref)
    flat_ref[...] = flat
    blocks = jnp.dot(selector.astype(jnp.bfloat16), flat, preferred_element_type=jnp.float32)
    per = steps * CAP
    for e in range(EXPERTS):
        for g in range(2):
            piece = blocks[e * per : (e + 1) * per, g * half : (g + 1) * half]
            send_ref[2 * e + g] = piece.astype(jnp.bfloat16)


def pack_tokens(tokens, expert_ids):
    steps, tok_count, width = tokens.shape
    return pl.pallas_call(
        pack_kernel,
        out_shape=(
            jax.ShapeDtypeStruct((2 * EXPERTS, steps * CAP, width // 2), jnp.bfloat16),
            jax.ShapeDtypeStruct((steps * tok_count, width), jnp.bfloat16),
        ),
        in_specs=[anywhere(), anywhere()],
        out_specs=(in_vmem(), in_vmem()),
        scratch_shapes=[
            pltpu.SMEM(expert_ids.shape, jnp.int32),
            pltpu.VMEM(tokens.shape, jnp.bfloat16),
            pltpu.SemaphoreType.DMA((2,)),
        ],
        name="pack_tokens",
        **vm_params(10**6, 10**6),
    )(expert_ids, tokens)


def up_copies(up_ref, held_ref, sems, first):
    depth = held_ref.shape[1]
    return [
        pltpu.make_async_copy(
            up_ref.at[pl.ds(first, depth), :, pl.ds(c * 128, 128)], held_ref.at[c], sems.at[c]
        )
        for c in range(held_ref.shape[0])
    ]


def rows_in_turn(held):
    return held.reshape(held.shape[0], -1, 128)


def spread_matrix():
    row = lax.broadcasted_iota(jnp.int32, (128, 512), 0)
    col = lax.broadcasted_iota(jnp.int32, (128, 512), 1)
    target = jnp.where(col < 256, 2 * row, 2 * row + 257)
    return jnp.where(col == target, 1.0, 0.0).astype(jnp.bfloat16)


def spread_rows(x_ref, spread_ref):
    rows, width = x_ref.shape
    batch = math.gcd(width // 128, 14 if rows <= 16 else 4)
    matrix = spread_matrix()

    def step(i, carry):
        at = pl.multiple_of(i * 128 * batch, 128 * batch)
        chunk = jnp.concatenate(
            [x_ref[:, pl.ds(at + 128 * b, 128)] for b in range(batch)], axis=0
        )
        wide = jnp.dot(chunk, matrix, preferred_element_type=jnp.float32).astype(jnp.bfloat16)
        to = pl.multiple_of(i * 256 * batch, 256 * batch)
        for b in range(batch):
            piece = wide[b * rows : (b + 1) * rows]
            spread_ref[0:rows, pl.ds(to + 256 * b, 256)] = piece[:, :256]
            spread_ref[rows : 2 * rows, pl.ds(to + 256 * b, 256)] = piece[:, 256:]
        return carry

    lax.fori_loop(0, width // (128 * batch), step, 0)


def up_matmul(spread_ref, up_ref, acc_ref):
    depth = spread_ref.shape[1]
    chunk = math.gcd(depth, UP_ROWS)

    def step(i, carry):
        src = pl.ds(pl.multiple_of(i * chunk, chunk), chunk)
        rows = spread_ref[:, src]
        for p in range(up_ref.shape[0] // 2):
            pair = jnp.concatenate([up_ref[2 * p, src, :], up_ref[2 * p + 1, src, :]], axis=1)
            acc_ref[:, p * 256 : (p + 1) * 256] += jnp.dot(
                rows, pair, preferred_element_type=jnp.float32
            )
        return carry

    lax.fori_loop(0, depth // chunk, step, 0)


def hidden_of(acc_ref):
    rows = acc_ref.shape[0] // 2
    gate, up = acc_ref[0:rows], acc_ref[rows : 2 * rows]
    return (jax.nn.silu(gate) * up).astype(jnp.bfloat16)


def down_matmul(hidden, down_ref, first, out_ref, chunk):
    def step(i, carry):
        at = pl.multiple_of(i * chunk, chunk)
        out_ref[:, pl.ds(at, chunk)] = jnp.dot(
            hidden[...],
            down_ref[:, pl.ds(pl.multiple_of(first + at, chunk), chunk)],
            preferred_element_type=jnp.float32,
        ).astype(out_ref.dtype)
        return carry

    lax.fori_loop(0, out_ref.shape[1] // chunk, step, 0)


def flatten_rows(block_ref, flat_ref):
    sources, per, _ = block_ref.shape
    group = max(1, 16 // per)
    for i in range(0, sources, group):
        rows = jnp.concatenate(
            [block_ref[i + j].astype(jnp.float32) for j in range(group)], axis=0
        )
        flat_ref[i * per : (i + group) * per] = rows.astype(flat_ref.dtype)


def half_fetch_kernel(block_ref, up_ref, held_ref, spread_ref, sems, flat_ref):
    copies = up_copies(up_ref, held_ref, sems, core_side() * held_ref.shape[1])
    for copy in copies:
        copy.start()
    flatten_rows(block_ref, flat_ref)
    spread_rows(flat_ref, spread_ref)
    for copy in copies:
        copy.wait()


def first_up_kernel(ready_ref, spread_ref, block_ref, up_ref, held_ref, next_ref, acc_ref, sems,
                    flat_ref):
    copies = up_copies(up_ref, held_ref, sems, (1 - core_side()) * held_ref.shape[1])
    for copy in copies:
        copy.start()
    flatten_rows(block_ref, flat_ref)
    spread_rows(flat_ref, next_ref)
    acc_ref[...] = jnp.zeros_like(acc_ref)
    up_matmul(spread_ref, ready_ref, acc_ref)
    for copy in copies:
        copy.wait()


def second_up_kernel(ready_ref, spread_ref, part_ref, down_ref, hid_ref, held_ref, out_ref, sems,
                     acc_ref):
    half = out_ref.shape[1]
    chunk = half // DOWN_PIECES
    side = core_side()

    def piece(first, i):
        at = pl.ds(pl.multiple_of(first + i * chunk, chunk), chunk)
        return pltpu.make_async_copy(down_ref.at[:, at], held_ref.at[:, at], sems.at[i])

    theirs = [piece((1 - side) * half, i) for i in range(DOWN_PIECES)]
    mine = pl.ds(pl.multiple_of(side * half, half), half)
    rest = pltpu.make_async_copy(
        down_ref.at[:, mine], held_ref.at[:, mine], sems.at[DOWN_PIECES]
    )
    for copy in theirs:
        copy.start()
    rest.start()
    acc_ref[...] = part_ref[...]
    up_matmul(spread_ref, ready_ref, acc_ref)
    hid_ref[...] = hidden_of(acc_ref)
    for i, copy in enumerate(theirs):
        copy.wait()
        at = pl.ds(pl.multiple_of((1 - side) * half + i * chunk, chunk), chunk)
        out_ref[:, i * chunk : (i + 1) * chunk] = jnp.dot(
            hid_ref[...], held_ref[:, at], preferred_element_type=jnp.float32
        ).astype(out_ref.dtype)
    rest.wait()


def own_down_kernel(hid_ref, down_ref, out_ref):
    half = out_ref.shape[1]
    down_matmul(hid_ref, down_ref, core_side() * half, out_ref, half // 2)


def routed_part(mine, up, down, swap):
    sources, per, half = mine.shape
    rows, hidden = sources * per, down.shape[0]
    tiles = hidden // 128
    held_half = pltpu.VMEM((tiles, half, 2, 128), jnp.bfloat16)
    spread = pltpu.VMEM((2 * rows, 2 * half), jnp.bfloat16)
    sems = pltpu.SemaphoreType.DMA((tiles,))
    flat = pltpu.VMEM((rows, half), jnp.bfloat16)
    theirs = swap(mine)
    held, spread_mine = pl.pallas_call(
        half_fetch_kernel,
        out_shape=(held_half, spread),
        in_specs=[in_vmem(), anywhere()],
        out_specs=(in_vmem(), in_vmem()),
        scratch_shapes=[sems, flat],
        name="half_fetch",
        **vm_params(0, up.size),
    )(mine, up)
    held, spread_theirs, part = pl.pallas_call(
        first_up_kernel,
        out_shape=(
            held_half, spread, pltpu.VMEM((2 * rows, hidden), jnp.float32)
        ),
        in_specs=[in_vmem()] * 3 + [anywhere()],
        out_specs=(in_vmem(),) * 3,
        scratch_shapes=[sems, flat],
        name="first_up",
        **vm_params(8 * rows * half * hidden, up.size),
    )(rows_in_turn(held), spread_mine, theirs, up)
    hid, down_held, sent = pl.pallas_call(
        second_up_kernel,
        out_shape=(
            pltpu.VMEM((rows, hidden), jnp.bfloat16),
            pltpu.VMEM(down.shape, jnp.bfloat16),
            jax.ShapeDtypeStruct((rows, half), jnp.bfloat16),
        ),
        in_specs=[in_vmem()] * 3 + [anywhere()],
        out_specs=(in_vmem(),) * 3,
        scratch_shapes=[
            pltpu.SemaphoreType.DMA((DOWN_PIECES + 1,)),
            pltpu.VMEM((2 * rows, hidden), jnp.float32),
        ],
        name="second_up",
        **vm_params(10 * rows * half * hidden, 2 * down.size),
    )(rows_in_turn(held), spread_theirs, part, down)
    got = swap(sent)
    kept = pl.pallas_call(
        own_down_kernel,
        out_shape=pltpu.VMEM((rows, half), jnp.float32),
        in_specs=[in_vmem()] * 2,
        out_specs=in_vmem(),
        name="own_down",
        **vm_params(2 * rows * half * hidden, 10**7),
    )(hid, down_held)
    return pl.pallas_call(
        add_kernel,
        out_shape=jax.ShapeDtypeStruct(mine.shape, jnp.bfloat16),
        in_specs=[in_vmem()] * 2,
        out_specs=in_vmem(),
        name="add_halves",
        **vm_params(rows * half, 10**6),
    )(kept, got)


def add_kernel(kept_ref, got_ref, out_ref):
    total = kept_ref[...] + got_ref[...].astype(jnp.float32)
    per = out_ref.shape[1]
    for i in range(out_ref.shape[0]):
        out_ref[i] = total[i * per : (i + 1) * per].astype(jnp.bfloat16)


def join_rows(mine_ref, theirs_ref, first, flat_ref):
    rows, depth = flat_ref.shape
    flat_ref[0 : rows // 2] = mine_ref[:, first : first + depth]
    flat_ref[rows // 2 : rows] = theirs_ref[:, first : first + depth]


def shared_fetch_kernel(mine_ref, theirs_ref, up_ref, held_ref, spread_ref, sems, flat_ref):
    copies = up_copies(up_ref, held_ref, sems, 0)
    for copy in copies:
        copy.start()
    join_rows(mine_ref, theirs_ref, 0, flat_ref)
    spread_rows(flat_ref, spread_ref)
    for copy in copies:
        copy.wait()


def shared_first_kernel(ready_ref, spread_ref, mine_ref, theirs_ref, up_ref, held_ref, next_ref,
                        last_ref, acc_ref, sems, flat_ref, end_ref):
    depth = held_ref.shape[1]
    copies = up_copies(up_ref, held_ref, sems, depth)
    for copy in copies:
        copy.start()
    join_rows(mine_ref, theirs_ref, depth, flat_ref)
    spread_rows(flat_ref, next_ref)
    join_rows(mine_ref, theirs_ref, 2 * depth, end_ref)
    spread_rows(end_ref, last_ref)
    acc_ref[...] = jnp.zeros_like(acc_ref)
    up_matmul(spread_ref, ready_ref, acc_ref)
    for copy in copies:
        copy.wait()


def shared_second_kernel(ready_ref, spread_ref, part_ref, acc_ref):
    acc_ref[...] = part_ref[...]
    up_matmul(spread_ref, ready_ref, acc_ref)


def shared_start(mine, theirs, up):
    width, _, hidden = up.shape
    rows, tiles = 2 * mine.shape[0], hidden // 128
    depth = 3 * width // 8
    held_piece = pltpu.VMEM((tiles, depth, 2, 128), jnp.bfloat16)
    spread = pltpu.VMEM((2 * rows, 2 * depth), jnp.bfloat16)
    last = jax.ShapeDtypeStruct((2 * rows, 2 * (width - 2 * depth)), jnp.bfloat16)
    sums = (2 * rows, hidden)
    sems = pltpu.SemaphoreType.DMA((tiles,))
    flat = pltpu.VMEM((rows, depth), jnp.bfloat16)
    held, spread_now = pl.pallas_call(
        shared_fetch_kernel,
        out_shape=(held_piece, spread),
        in_specs=[in_vmem(), in_vmem(), anywhere()],
        out_specs=(in_vmem(), in_vmem()),
        scratch_shapes=[sems, flat],
        name="shared_fetch",
        **vm_params(0, up.size),
    )(mine, theirs, up)
    held, spread_now, spread_last, part = pl.pallas_call(
        shared_first_kernel,
        out_shape=(held_piece, spread, last, pltpu.VMEM(sums, jnp.float32)),
        in_specs=[in_vmem()] * 4 + [anywhere()],
        out_specs=(in_vmem(),) * 4,
        scratch_shapes=[sems, flat, pltpu.VMEM((rows, width - 2 * depth), jnp.bfloat16)],
        name="shared_first",
        **vm_params(0, up.size),
    )(rows_in_turn(held), spread_now, mine, theirs, up)
    part = pl.pallas_call(
        shared_second_kernel,
        out_shape=jax.ShapeDtypeStruct(sums, jnp.float32),
        in_specs=[in_vmem()] * 3,
        out_specs=in_vmem(),
        name="shared_second",
        **vm_params(0, up.size // 2),
    )(rows_in_turn(held), spread_now, part)
    return part, spread_last


def shared_last_kernel(part_ref, up_ref, held_ref, sems):
    del part_ref
    depth = held_ref.shape[1]
    copies = up_copies(up_ref, held_ref, sems, up_ref.shape[0] - depth)
    for copy in copies:
        copy.start()
    for copy in copies:
        copy.wait()


def shared_down_kernel(ready_ref, spread_ref, part_ref, ids_ref, gates_ref, down_ref, mine_ref,
                       theirs_ref, weight_ref, acc_ref, held_ref, sems):
    count, _, chunk = held_ref.shape
    rows = mine_ref.shape[0]
    copies = [
        pltpu.make_async_copy(
            down_ref.at[:, pl.ds(i * chunk, chunk)], held_ref.at[i], sems.at[i]
        )
        for i in range(count)
    ]
    for copy in copies:
        copy.start()
    weight_ref[...] = slot_weights(ids_ref, gates_ref)
    acc_ref[...] = part_ref[...]
    up_matmul(spread_ref, ready_ref, acc_ref)
    hid = hidden_of(acc_ref)
    for i, copy in enumerate(copies):
        copy.wait()
        part = jnp.dot(hid, held_ref[i], preferred_element_type=jnp.float32)
        cols = slice(i * chunk, (i + 1) * chunk)
        mine_ref[:, cols] = part[0:rows]
        theirs_ref[:, cols] = part[rows : 2 * rows].astype(jnp.bfloat16)


def shared_finish(part, spread_last, up, down, ids, gates):
    rows, (hidden, width) = part.shape[0] // 4, down.shape
    tiles, depth, chunk = hidden // 128, spread_last.shape[1] // 2, width // (2 * DOWN_PIECES)
    _, steps, tok_count = ids.shape
    held = pl.pallas_call(
        shared_last_kernel,
        out_shape=pltpu.VMEM((tiles, depth, 2, 128), jnp.bfloat16),
        in_specs=[anywhere(), anywhere()],
        out_specs=in_vmem(),
        scratch_shapes=[pltpu.SemaphoreType.DMA((tiles,))],
        name="shared_last",
        **vm_params(0, up.size // 2),
    )(part, up)
    return pl.pallas_call(
        shared_down_kernel,
        out_shape=(
            jax.ShapeDtypeStruct((rows, width), jnp.float32),
            jax.ShapeDtypeStruct((rows, width), jnp.bfloat16),
            jax.ShapeDtypeStruct((steps * tok_count, EXPERTS * steps * CAP), jnp.bfloat16),
        ),
        in_specs=[in_vmem()] * 3 + [in_smem(), in_smem(), anywhere()],
        out_specs=(in_vmem(),) * 3,
        scratch_shapes=[
            pltpu.VMEM(part.shape, jnp.float32),
            pltpu.VMEM((2 * DOWN_PIECES, hidden, chunk), jnp.bfloat16),
            pltpu.SemaphoreType.DMA((2 * DOWN_PIECES,)),
        ],
        name="shared_down",
        compiler_params=pltpu.CompilerParams(vmem_limit_bytes=3 * VMEM_GRANT),
        cost_estimate=pl.CostEstimate(
            flops=0, bytes_accessed=2 * down.size, transcendentals=0
        ),
    )(rows_in_turn(held), spread_last, part, ids, gates, down)


def slot_weights(ids_ref, gates_ref):
    _, steps, tok_count = ids_ref.shape
    rows, slots = steps * tok_count, EXPERTS * steps * CAP
    place = lax.broadcasted_iota(jnp.int32, (rows, slots), 0) * slots + lax.broadcasted_iota(
        jnp.int32, (rows, slots), 1
    )
    weights = jnp.zeros((rows, slots), jnp.float32)
    for (s, t, k), number in slot_numbers(ids_ref).items():
        weights = jnp.where(
            place == (s * tok_count + t) * slots + number, gates_ref[k, s, t], weights
        )
    return weights.astype(jnp.bfloat16)


def combine_kernel(weight_ref, back_ref, kept_ref, got_ref, out_ref):
    steps, tok_count, width = out_ref.shape
    half = width // 2
    weights = weight_ref[...]
    for g in range(2):
        parts = jnp.concatenate(
            [back_ref[2 * e + g].astype(jnp.float32) for e in range(EXPERTS)], axis=0
        ).astype(jnp.bfloat16)
        total = jnp.dot(weights, parts, preferred_element_type=jnp.float32)
        cols = slice(g * half, (g + 1) * half)
        total = total + (kept_ref[:, cols] + got_ref[:, cols].astype(jnp.float32))
        for s in range(steps):
            out_ref[s, :, cols] = total[s * tok_count : (s + 1) * tok_count].astype(jnp.bfloat16)


def combine(weights, back, kept, got, like):
    return pl.pallas_call(
        combine_kernel,
        out_shape=jax.ShapeDtypeStruct(like.shape, jnp.bfloat16),
        in_specs=[in_vmem()] * 4,
        out_specs=in_vmem(),
        name="combine",
        **vm_params(10**6, 10**6),
    )(weights, back, kept, got)


def by_chip(tokens, expert_ids, gate_weights, w_gate_up, w_down, shared_gate_up, shared_down):
    pairs = [(i, i ^ 1) for i in range(lax.axis_size("fast"))]

    def swap(x):
        return lax.ppermute(x, "fast", pairs)

    def exchange(x):
        return lax.all_to_all(x, "fast", split_axis=0, concat_axis=0, tiled=True)

    gates = jnp.transpose(gate_weights, (2, 0, 1)).astype(jnp.float32)
    expert_ids = jnp.transpose(expert_ids, (2, 0, 1))
    weights = (w_gate_up, w_down, shared_gate_up, shared_down)
    w_gate_up, w_down, shared_gate_up, shared_down = (in_hbm(w) for w in weights)
    send, flat = pack_tokens(in_hbm(tokens), in_hbm(expert_ids))
    arrived = exchange(send)
    part, spread_last = shared_start(flat, swap(flat), shared_gate_up)
    arrived, part = lax.optimization_barrier((arrived, part))
    partials = routed_part(arrived, w_gate_up, w_down, swap)
    partials, part = lax.optimization_barrier((partials, part))
    back = exchange(partials)
    kept, sent, slots = shared_finish(
        part, spread_last, shared_gate_up, shared_down, expert_ids, gates
    )
    return combine(slots, back, kept, swap(sent), tokens)


def solution(mesh):
    placed = (
        P(None, ("rep", "fast"), None),
        P(None, ("rep", "fast"), None),
        P(None, ("rep", "fast"), None),
        P(None, None, "fast"),
        P("fast", None),
        P(None, None, "fast"),
        P("fast", None),
    )
    return jax.shard_map(
        local, mesh=mesh, in_specs=placed, out_specs=P(None, ("rep", "fast"), None), check_vma=False
    )
```

```python
import functools
import math

import jax
import jax.numpy as jnp
from jax import lax
from jax.experimental import pallas as pl
from jax.experimental.pallas import tpu as pltpu
from jax.sharding import PartitionSpec as P

EXPERTS = 8
TOPK = 3
STEPS = 2
CAP = 2
VMEM_GRANT = 8 * 2**20
DOWN_PIECES = 7
UP_ROWS = 7 * 256


def slot_tables(step_tokens, step_ids, step_gates):
    tok_count = step_ids.shape[0]
    flat_ids = step_ids.reshape(tok_count * TOPK)
    expert_hit = (flat_ids[:, None] == jnp.arange(EXPERTS, dtype=jnp.int32)[None, :]).astype(
        jnp.int32
    )
    slot_rank = jnp.sum((jnp.cumsum(expert_hit, axis=0) - expert_hit) * expert_hit, axis=1)
    slot_index = flat_ids * CAP + slot_rank
    placed = (slot_index[:, None] == jnp.arange(EXPERTS * CAP, dtype=jnp.int32)[None, :]).astype(
        jnp.float32
    )
    selector = jnp.sum(placed.reshape(tok_count, TOPK, EXPERTS * CAP), axis=1)
    blocks = jnp.einsum(
        "ts,td->sd", selector.astype(jnp.bfloat16), step_tokens, preferred_element_type=jnp.float32
    ).astype(jnp.bfloat16)
    share_row = jnp.broadcast_to(
        (jnp.arange(TOPK) == 0).astype(jnp.float32)[None, :], (tok_count, TOPK)
    ).reshape(-1)
    gate_row = step_gates.astype(jnp.float32).reshape(-1)
    slot_coefs = jnp.einsum(
        "rs,rc->sc",
        placed,
        jnp.stack([gate_row, share_row], axis=1),
        precision=lax.Precision.HIGHEST,
    ).astype(jnp.bfloat16)
    return (blocks.reshape(EXPERTS, CAP, -1), slot_coefs.reshape(EXPERTS, CAP, 2), selector)


def send_out(blocks, slot_coefs, group_size):
    spread = jnp.repeat(blocks, group_size, axis=0)
    spread_coefs = jnp.repeat(slot_coefs, group_size, axis=0)
    arrived, arrived_coefs = (
        lax.all_to_all(spread, "fast", split_axis=0, concat_axis=0, tiled=True),
        lax.all_to_all(spread_coefs, "fast", split_axis=0, concat_axis=0, tiled=True),
    )
    return (arrived, arrived_coefs)


def expert_work(arrived, arrived_coefs, weights):
    w_gate_up, w_down, shared_gate_up, shared_down = weights
    model_width = arrived.shape[-1]
    hidden_size = w_down.shape[0]
    flat_rows = arrived.reshape(-1, model_width)
    flat_coef = arrived_coefs.reshape(-1, 2).astype(jnp.float32)
    row_count = flat_rows.shape[0]
    block_rows = math.gcd(row_count, 512)
    routed_up = w_gate_up.reshape(model_width, 2 * hidden_size)
    common_up = shared_gate_up.reshape(model_width, 2 * hidden_size)

    def one_block(block_pair):
        row_block, slot_coef = block_pair
        routed = jnp.dot(row_block, routed_up, preferred_element_type=jnp.float32)
        routed_hidden = (jax.nn.silu(routed[:, :hidden_size]) * routed[:, hidden_size:]).astype(
            jnp.bfloat16
        )
        common = jnp.dot(row_block, common_up, preferred_element_type=jnp.float32)
        common_hidden = (jax.nn.silu(common[:, :hidden_size]) * common[:, hidden_size:]).astype(
            jnp.bfloat16
        )
        result = slot_coef[:, 0:1] * jnp.dot(
            routed_hidden, w_down, preferred_element_type=jnp.float32
        )
        result = result + slot_coef[:, 1:2] * jnp.dot(
            common_hidden, shared_down, preferred_element_type=jnp.float32
        )
        return result.astype(jnp.bfloat16)

    outcome = lax.map(
        one_block,
        (flat_rows.reshape(-1, block_rows, model_width), flat_coef.reshape(-1, block_rows, 2)),
    )
    return outcome.reshape(arrived.shape)


def round_trip(blocks, slot_coefs, weights, group_size):
    arrived, arrived_coefs = send_out(blocks, slot_coefs, group_size)
    partials = expert_work(arrived, arrived_coefs, weights)
    returned = lax.all_to_all(partials, "fast", split_axis=0, concat_axis=0, tiled=True)
    slot_count = blocks.shape[1]
    return returned.reshape(EXPERTS, group_size, slot_count, -1).astype(jnp.float32).sum(axis=1)


def finish(selector, summed):
    flat_sums = summed.reshape(selector.shape[1], -1)
    return jnp.dot(
        selector, flat_sums, precision=lax.Precision.HIGHEST, preferred_element_type=jnp.float32
    ).astype(jnp.bfloat16)


def local(tokens, expert_ids, gate_weights, w_gate_up, w_down, shared_gate_up, shared_down):
    group_size = lax.axis_size("fast") // EXPERTS
    if group_size == 2 and w_down.shape[0] % 256 == 0 and tokens.shape[-1] % (DOWN_PIECES * 1024) == 0:
        return by_chip(
            tokens, expert_ids, gate_weights, w_gate_up, w_down, shared_gate_up, shared_down
        )
    weights = (w_gate_up, w_down, shared_gate_up, shared_down)
    prepared = [
        slot_tables(tokens[step_index], expert_ids[step_index], gate_weights[step_index])
        for step_index in range(STEPS)
    ]
    outputs = []
    model_width = tokens.shape[-1]
    blocks = jnp.stack([member[0] for member in prepared], axis=1).reshape(
        EXPERTS, STEPS * CAP, model_width
    )
    slot_coefs = jnp.stack([member[1] for member in prepared], axis=1).reshape(
        EXPERTS, STEPS * CAP, 2
    )
    summed = round_trip(blocks, slot_coefs, weights, group_size).reshape(
        EXPERTS, STEPS, CAP, model_width
    )
    for step_index in range(STEPS):
        outputs.append(finish(prepared[step_index][2], summed[:, step_index]))
    return jnp.stack(outputs, axis=0)


def vm_params(flops=0, moved=0):
    return dict(
        compiler_params=pltpu.CompilerParams(vmem_limit_bytes=VMEM_GRANT),
        cost_estimate=pl.CostEstimate(flops=flops, bytes_accessed=moved, transcendentals=0),
    )


def in_vmem():
    return pl.BlockSpec(memory_space=pltpu.VMEM)


def in_smem():
    return pl.BlockSpec(memory_space=pltpu.SMEM)


def anywhere():
    return pl.BlockSpec(memory_space=pltpu.HBM)


def in_hbm(x):
    return pltpu.with_memory_space_constraint(x, pltpu.HBM)


def core_side():
    return lax.rem(lax.axis_index("fast"), 2)


def slot_numbers(ids_ref):
    choices, steps, tok_count = ids_ref.shape
    numbers = {}
    for s in range(steps):
        ids = [[ids_ref[k, s, t] for k in range(choices)] for t in range(tok_count)]
        for t in range(tok_count):
            for k in range(choices):
                rank = jnp.int32(0)
                for earlier in range(t):
                    for other in ids[earlier]:
                        rank = rank + (other == ids[t][k]).astype(jnp.int32)
                numbers[s, t, k] = ids[t][k] * (steps * CAP) + s * CAP + rank
    return numbers


def stacked_tokens(tok_ref):
    parts = [tok_ref[s].astype(jnp.float32) for s in range(tok_ref.shape[0])]
    return jnp.concatenate(parts, axis=0).astype(jnp.bfloat16)


def pack_kernel(ids_hbm, tok_hbm, send_ref, flat_ref, ids_ref, tok_ref, sems):
    copies = [
        pltpu.make_async_copy(ids_hbm, ids_ref, sems.at[0]),
        pltpu.make_async_copy(tok_hbm, tok_ref, sems.at[1]),
    ]
    for copy in copies:
        copy.start()
    steps, tok_count, width = tok_ref.shape
    rows, slots = steps * tok_count, EXPERTS * steps * CAP
    half = width // 2
    copies[0].wait()
    numbers = slot_numbers(ids_ref)
    place = lax.broadcasted_iota(jnp.int32, (slots, rows), 0) * rows + lax.broadcasted_iota(
        jnp.int32, (slots, rows), 1
    )
    selector = jnp.zeros((slots, rows), jnp.float32)
    for (s, t, k), number in numbers.items():
        selector = jnp.where(place == number * rows + (s * tok_count + t), 1.0, selector)
    copies[1].wait()
    flat = stacked_tokens(tok_ref)
    flat_ref[...] = flat
    blocks = jnp.dot(selector.astype(jnp.bfloat16), flat, preferred_element_type=jnp.float32)
    per = steps * CAP
    for e in range(EXPERTS):
        for g in range(2):
            piece = blocks[e * per : (e + 1) * per, g * half : (g + 1) * half]
            send_ref[2 * e + g] = piece.astype(jnp.bfloat16)


def pack_tokens(tokens, expert_ids):
    steps, tok_count, width = tokens.shape
    return pl.pallas_call(
        pack_kernel,
        out_shape=(
            jax.ShapeDtypeStruct((2 * EXPERTS, steps * CAP, width // 2), jnp.bfloat16),
            jax.ShapeDtypeStruct((steps * tok_count, width), jnp.bfloat16),
        ),
        in_specs=[anywhere(), anywhere()],
        out_specs=(in_vmem(), in_vmem()),
        scratch_shapes=[
            pltpu.SMEM(expert_ids.shape, jnp.int32),
            pltpu.VMEM(tokens.shape, jnp.bfloat16),
            pltpu.SemaphoreType.DMA((2,)),
        ],
        name="pack_tokens",
        **vm_params(10**6, 10**6),
    )(expert_ids, tokens)


def up_copies(up_ref, held_ref, sems, first):
    depth = held_ref.shape[1]
    return [
        pltpu.make_async_copy(
            up_ref.at[pl.ds(first, depth), :, pl.ds(c * 128, 128)], held_ref.at[c], sems.at[c]
        )
        for c in range(held_ref.shape[0])
    ]


def rows_in_turn(held):
    return held.reshape(held.shape[0], -1, 128)


def spread_matrix():
    row = lax.broadcasted_iota(jnp.int32, (128, 512), 0)
    col = lax.broadcasted_iota(jnp.int32, (128, 512), 1)
    target = jnp.where(col < 256, 2 * row, 2 * row + 257)
    return jnp.where(col == target, 1.0, 0.0).astype(jnp.bfloat16)


def spread_rows(x_ref, spread_ref):
    rows, width = x_ref.shape
    batch = math.gcd(width // 128, 14 if rows <= 16 else 4)
    matrix = spread_matrix()

    def step(i, carry):
        at = pl.multiple_of(i * 128 * batch, 128 * batch)
        chunk = jnp.concatenate(
            [x_ref[:, pl.ds(at + 128 * b, 128)] for b in range(batch)], axis=0
        )
        wide = jnp.dot(chunk, matrix, preferred_element_type=jnp.float32).astype(jnp.bfloat16)
        to = pl.multiple_of(i * 256 * batch, 256 * batch)
        for b in range(batch):
            piece = wide[b * rows : (b + 1) * rows]
            spread_ref[0:rows, pl.ds(to + 256 * b, 256)] = piece[:, :256]
            spread_ref[rows : 2 * rows, pl.ds(to + 256 * b, 256)] = piece[:, 256:]
        return carry

    lax.fori_loop(0, width // (128 * batch), step, 0)


def up_matmul(spread_ref, up_ref, acc_ref):
    depth = spread_ref.shape[1]
    chunk = math.gcd(depth, UP_ROWS)

    def step(i, carry):
        src = pl.ds(pl.multiple_of(i * chunk, chunk), chunk)
        rows = spread_ref[:, src]
        for p in range(up_ref.shape[0] // 2):
            pair = jnp.concatenate([up_ref[2 * p, src, :], up_ref[2 * p + 1, src, :]], axis=1)
            acc_ref[:, p * 256 : (p + 1) * 256] += jnp.dot(
                rows, pair, preferred_element_type=jnp.float32
            )
        return carry

    lax.fori_loop(0, depth // chunk, step, 0)


def hidden_of(acc_ref):
    rows = acc_ref.shape[0] // 2
    gate, up = acc_ref[0:rows], acc_ref[rows : 2 * rows]
    return (jax.nn.silu(gate) * up).astype(jnp.bfloat16)


def flatten_rows(block_ref, flat_ref):
    sources, per, _ = block_ref.shape
    group = max(1, 16 // per)
    for i in range(0, sources, group):
        rows = jnp.concatenate(
            [block_ref[i + j].astype(jnp.float32) for j in range(group)], axis=0
        )
        flat_ref[i * per : (i + group) * per] = rows.astype(flat_ref.dtype)


def half_fetch_kernel(block_ref, up_ref, held_ref, spread_ref, sems, flat_ref):
    copies = up_copies(up_ref, held_ref, sems, core_side() * held_ref.shape[1])
    for copy in copies:
        copy.start()
    flatten_rows(block_ref, flat_ref)
    spread_rows(flat_ref, spread_ref)
    for copy in copies:
        copy.wait()


def first_up_kernel(ready_ref, spread_ref, block_ref, up_ref, held_ref, next_ref, acc_ref, sems,
                    flat_ref):
    copies = up_copies(up_ref, held_ref, sems, (1 - core_side()) * held_ref.shape[1])
    for copy in copies:
        copy.start()
    flatten_rows(block_ref, flat_ref)
    spread_rows(flat_ref, next_ref)
    acc_ref[...] = jnp.zeros_like(acc_ref)
    up_matmul(spread_ref, ready_ref, acc_ref)
    for copy in copies:
        copy.wait()


def second_up_kernel(ready_ref, spread_ref, part_ref, down_ref, hid_ref, held_ref, out_ref, sems,
                     acc_ref):
    half = out_ref.shape[1]
    chunk = half // DOWN_PIECES
    side = core_side()

    def piece(first, i):
        at = pl.ds(pl.multiple_of(first + i * chunk, chunk), chunk)
        return pltpu.make_async_copy(down_ref.at[:, at], held_ref.at[:, at], sems.at[i])

    theirs = [piece((1 - side) * half, i) for i in range(DOWN_PIECES)]
    mine = pl.ds(pl.multiple_of(side * half, half), half)
    rest = pltpu.make_async_copy(
        down_ref.at[:, mine], held_ref.at[:, mine], sems.at[DOWN_PIECES]
    )
    for copy in theirs:
        copy.start()
    rest.start()
    acc_ref[...] = part_ref[...]
    up_matmul(spread_ref, ready_ref, acc_ref)
    hid_ref[...] = hidden_of(acc_ref)
    for i, copy in enumerate(theirs):
        copy.wait()
        at = pl.ds(pl.multiple_of((1 - side) * half + i * chunk, chunk), chunk)
        out_ref[:, i * chunk : (i + 1) * chunk] = jnp.dot(
            hid_ref[...], held_ref[:, at], preferred_element_type=jnp.float32
        ).astype(out_ref.dtype)
    rest.wait()


def own_down_kernel(hid_ref, down_ref, out_ref):
    half = out_ref.shape[1]
    first = core_side() * half
    for at in (0, half // 2):
        out_ref[:, at : at + half // 2] = jnp.dot(
            hid_ref[...],
            down_ref[:, pl.ds(pl.multiple_of(first + at, 256), half // 2)],
            preferred_element_type=jnp.float32,
        )


def routed_part(mine, up, down, swap):
    sources, per, half = mine.shape
    rows, hidden = sources * per, down.shape[0]
    tiles = hidden // 128
    held_half = pltpu.VMEM((tiles, half, 2, 128), jnp.bfloat16)
    spread = pltpu.VMEM((2 * rows, 2 * half), jnp.bfloat16)
    sems = pltpu.SemaphoreType.DMA((tiles,))
    flat = pltpu.VMEM((rows, half), jnp.bfloat16)
    theirs = swap(mine)
    held, spread_mine = pl.pallas_call(
        half_fetch_kernel,
        out_shape=(held_half, spread),
        in_specs=[in_vmem(), anywhere()],
        out_specs=(in_vmem(), in_vmem()),
        scratch_shapes=[sems, flat],
        name="half_fetch",
        **vm_params(0, up.size),
    )(mine, up)
    held, spread_theirs, part = pl.pallas_call(
        first_up_kernel,
        out_shape=(
            held_half, spread, pltpu.VMEM((2 * rows, hidden), jnp.float32)
        ),
        in_specs=[in_vmem()] * 3 + [anywhere()],
        out_specs=(in_vmem(),) * 3,
        scratch_shapes=[sems, flat],
        name="first_up",
        **vm_params(8 * rows * half * hidden, up.size),
    )(rows_in_turn(held), spread_mine, theirs, up)
    hid, down_held, sent = pl.pallas_call(
        second_up_kernel,
        out_shape=(
            pltpu.VMEM((rows, hidden), jnp.bfloat16),
            pltpu.VMEM(down.shape, jnp.bfloat16),
            jax.ShapeDtypeStruct((rows, half), jnp.bfloat16),
        ),
        in_specs=[in_vmem()] * 3 + [anywhere()],
        out_specs=(in_vmem(),) * 3,
        scratch_shapes=[
            pltpu.SemaphoreType.DMA((DOWN_PIECES + 1,)),
            pltpu.VMEM((2 * rows, hidden), jnp.float32),
        ],
        name="second_up",
        **vm_params(10 * rows * half * hidden, 2 * down.size),
    )(rows_in_turn(held), spread_theirs, part, down)
    got = swap(sent)
    kept = pl.pallas_call(
        own_down_kernel,
        out_shape=pltpu.VMEM((rows, half), jnp.float32),
        in_specs=[in_vmem()] * 2,
        out_specs=in_vmem(),
        name="own_down",
        **vm_params(2 * rows * half * hidden, 10**7),
    )(hid, down_held)
    return pl.pallas_call(
        add_kernel,
        out_shape=jax.ShapeDtypeStruct(mine.shape, jnp.bfloat16),
        in_specs=[in_vmem()] * 2,
        out_specs=anywhere(),
        scratch_shapes=[
            pltpu.VMEM(mine.shape, jnp.bfloat16),
            pltpu.SemaphoreType.DMA((math.gcd(sources, 4),)),
        ],
        name="add_halves",
        **vm_params(rows * half, 10**6),
    )(kept, got)


def add_kernel(kept_ref, got_ref, out_hbm, out_ref, sems):
    count, per, _ = out_ref.shape
    group = count // sems.shape[0]
    copies = []
    for i in range(sems.shape[0]):
        rows = slice(i * group * per, (i + 1) * group * per)
        total = kept_ref[rows] + got_ref[rows].astype(jnp.float32)
        for j in range(group):
            out_ref[i * group + j] = total[j * per : (j + 1) * per].astype(jnp.bfloat16)
        part = pl.ds(i * group, group)
        copies.append(pltpu.make_async_copy(out_ref.at[part], out_hbm.at[part], sems.at[i]))
        copies[-1].start()
    for copy in copies:
        copy.wait()


def join_rows(mine_ref, theirs_ref, first, flat_ref):
    rows, depth = flat_ref.shape
    flat_ref[0 : rows // 2] = mine_ref[:, first : first + depth]
    flat_ref[rows // 2 : rows] = theirs_ref[:, first : first + depth]


def shared_fetch_kernel(mine_ref, theirs_ref, up_ref, held_ref, spread_ref, sems, flat_ref):
    copies = up_copies(up_ref, held_ref, sems, 0)
    for copy in copies:
        copy.start()
    join_rows(mine_ref, theirs_ref, 0, flat_ref)
    spread_rows(flat_ref, spread_ref)
    for copy in copies:
        copy.wait()


def shared_first_kernel(ready_ref, spread_ref, mine_ref, theirs_ref, up_ref, held_ref, next_ref,
                        last_ref, acc_ref, sems, flat_ref, end_ref):
    depth = held_ref.shape[1]
    copies = up_copies(up_ref, held_ref, sems, depth)
    for copy in copies:
        copy.start()
    join_rows(mine_ref, theirs_ref, depth, flat_ref)
    spread_rows(flat_ref, next_ref)
    join_rows(mine_ref, theirs_ref, 2 * depth, end_ref)
    spread_rows(end_ref, last_ref)
    acc_ref[...] = jnp.zeros_like(acc_ref)
    up_matmul(spread_ref, ready_ref, acc_ref)
    for copy in copies:
        copy.wait()


def shared_second_kernel(ready_ref, spread_ref, part_ref, acc_ref):
    acc_ref[...] = part_ref[...]
    up_matmul(spread_ref, ready_ref, acc_ref)


def shared_start(mine, theirs, up):
    width, _, hidden = up.shape
    rows, tiles = 2 * mine.shape[0], hidden // 128
    depth = 3 * width // 8
    held_piece = pltpu.VMEM((tiles, depth, 2, 128), jnp.bfloat16)
    spread = pltpu.VMEM((2 * rows, 2 * depth), jnp.bfloat16)
    last = jax.ShapeDtypeStruct((2 * rows, 2 * (width - 2 * depth)), jnp.bfloat16)
    sums = (2 * rows, hidden)
    sems = pltpu.SemaphoreType.DMA((tiles,))
    flat = pltpu.VMEM((rows, depth), jnp.bfloat16)
    held, spread_now = pl.pallas_call(
        shared_fetch_kernel,
        out_shape=(held_piece, spread),
        in_specs=[in_vmem(), in_vmem(), anywhere()],
        out_specs=(in_vmem(), in_vmem()),
        scratch_shapes=[sems, flat],
        name="shared_fetch",
        **vm_params(0, up.size),
    )(mine, theirs, up)
    held, spread_now, spread_last, part = pl.pallas_call(
        shared_first_kernel,
        out_shape=(held_piece, spread, last, pltpu.VMEM(sums, jnp.float32)),
        in_specs=[in_vmem()] * 4 + [anywhere()],
        out_specs=(in_vmem(),) * 4,
        scratch_shapes=[sems, flat, pltpu.VMEM((rows, width - 2 * depth), jnp.bfloat16)],
        name="shared_first",
        **vm_params(0, up.size),
    )(rows_in_turn(held), spread_now, mine, theirs, up)
    part = pl.pallas_call(
        shared_second_kernel,
        out_shape=jax.ShapeDtypeStruct(sums, jnp.float32),
        in_specs=[in_vmem()] * 3,
        out_specs=in_vmem(),
        name="shared_second",
        **vm_params(0, up.size // 2),
    )(rows_in_turn(held), spread_now, part)
    return part, spread_last


def shared_last_kernel(part_ref, up_ref, held_ref, sems):
    del part_ref
    depth = held_ref.shape[1]
    copies = up_copies(up_ref, held_ref, sems, up_ref.shape[0] - depth)
    for copy in copies:
        copy.start()
    for copy in copies:
        copy.wait()


def shared_down_kernel(ready_ref, spread_ref, part_ref, ids_ref, gates_ref, down_ref, mine_ref,
                       theirs_ref, weight_ref, acc_ref, held_ref, sems):
    count, _, chunk = held_ref.shape
    rows = mine_ref.shape[0]
    copies = [
        pltpu.make_async_copy(
            down_ref.at[:, pl.ds(i * chunk, chunk)], held_ref.at[i], sems.at[i]
        )
        for i in range(count)
    ]
    for copy in copies:
        copy.start()
    weight_ref[...] = slot_weights(ids_ref, gates_ref)
    acc_ref[...] = part_ref[...]
    up_matmul(spread_ref, ready_ref, acc_ref)
    hid = hidden_of(acc_ref)
    for i, copy in enumerate(copies):
        copy.wait()
        part = jnp.dot(hid, held_ref[i], preferred_element_type=jnp.float32)
        cols = slice(i * chunk, (i + 1) * chunk)
        mine_ref[:, cols] = part[0:rows]
        theirs_ref[:, cols] = part[rows : 2 * rows].astype(jnp.bfloat16)


def shared_finish(part, spread_last, up, down, ids, gates):
    rows, (hidden, width) = part.shape[0] // 4, down.shape
    tiles, depth, chunk = hidden // 128, spread_last.shape[1] // 2, width // (2 * DOWN_PIECES)
    _, steps, tok_count = ids.shape
    held = pl.pallas_call(
        shared_last_kernel,
        out_shape=pltpu.VMEM((tiles, depth, 2, 128), jnp.bfloat16),
        in_specs=[anywhere(), anywhere()],
        out_specs=in_vmem(),
        scratch_shapes=[pltpu.SemaphoreType.DMA((tiles,))],
        name="shared_last",
        **vm_params(0, up.size // 2),
    )(part, up)
    return pl.pallas_call(
        shared_down_kernel,
        out_shape=(
            jax.ShapeDtypeStruct((rows, width), jnp.float32),
            jax.ShapeDtypeStruct((rows, width), jnp.bfloat16),
            jax.ShapeDtypeStruct((steps * tok_count, EXPERTS * steps * CAP), jnp.bfloat16),
        ),
        in_specs=[in_vmem()] * 3 + [in_smem(), in_smem(), anywhere()],
        out_specs=(in_vmem(),) * 3,
        scratch_shapes=[
            pltpu.VMEM(part.shape, jnp.float32),
            pltpu.VMEM((2 * DOWN_PIECES, hidden, chunk), jnp.bfloat16),
            pltpu.SemaphoreType.DMA((2 * DOWN_PIECES,)),
        ],
        name="shared_down",
        compiler_params=pltpu.CompilerParams(vmem_limit_bytes=3 * VMEM_GRANT),
        cost_estimate=pl.CostEstimate(
            flops=0, bytes_accessed=2 * down.size, transcendentals=0
        ),
    )(rows_in_turn(held), spread_last, part, ids, gates, down)


def slot_weights(ids_ref, gates_ref):
    _, steps, tok_count = ids_ref.shape
    rows, slots = steps * tok_count, EXPERTS * steps * CAP
    place = lax.broadcasted_iota(jnp.int32, (rows, slots), 0) * slots + lax.broadcasted_iota(
        jnp.int32, (rows, slots), 1
    )
    weights = jnp.zeros((rows, slots), jnp.float32)
    for (s, t, k), number in slot_numbers(ids_ref).items():
        weights = jnp.where(
            place == (s * tok_count + t) * slots + number, gates_ref[k, s, t], weights
        )
    return weights.astype(jnp.bfloat16)


def combine_kernel(weight_ref, back_ref, kept_ref, got_ref, out_ref):
    steps, tok_count, width = out_ref.shape
    half = width // 2
    weights = weight_ref[...]
    for g in range(2):
        parts = jnp.concatenate(
            [back_ref[2 * e + g].astype(jnp.float32) for e in range(EXPERTS)], axis=0
        ).astype(jnp.bfloat16)
        total = jnp.dot(weights, parts, preferred_element_type=jnp.float32)
        cols = slice(g * half, (g + 1) * half)
        total = total + (kept_ref[:, cols] + got_ref[:, cols].astype(jnp.float32))
        for s in range(steps):
            out_ref[s, :, cols] = total[s * tok_count : (s + 1) * tok_count].astype(jnp.bfloat16)


def combine(weights, back, kept, got, like):
    return pl.pallas_call(
        combine_kernel,
        out_shape=jax.ShapeDtypeStruct(like.shape, jnp.bfloat16),
        in_specs=[in_vmem()] * 4,
        out_specs=in_vmem(),
        name="combine",
        **vm_params(10**6, 10**6),
    )(weights, back, kept, got)


def by_chip(tokens, expert_ids, gate_weights, w_gate_up, w_down, shared_gate_up, shared_down):
    pairs = [(i, i ^ 1) for i in range(lax.axis_size("fast"))]

    def swap(x):
        return lax.ppermute(x, "fast", pairs)

    def exchange(x):
        return lax.all_to_all(x, "fast", split_axis=0, concat_axis=0, tiled=True)

    gates = jnp.transpose(gate_weights, (2, 0, 1)).astype(jnp.float32)
    expert_ids = jnp.transpose(expert_ids, (2, 0, 1))
    weights = (w_gate_up, w_down, shared_gate_up, shared_down)
    w_gate_up, w_down, shared_gate_up, shared_down = (in_hbm(w) for w in weights)
    send, flat = pack_tokens(in_hbm(tokens), in_hbm(expert_ids))
    arrived = exchange(send)
    part, spread_last = shared_start(flat, swap(flat), shared_gate_up)
    arrived, part = lax.optimization_barrier((arrived, part))
    partials = routed_part(arrived, w_gate_up, w_down, swap)
    partials, part = lax.optimization_barrier((partials, part))
    back = exchange(partials)
    kept, sent, slots = shared_finish(
        part, spread_last, shared_gate_up, shared_down, expert_ids, gates
    )
    return combine(slots, back, kept, swap(sent), tokens)


def solution(mesh):
    placed = (
        P(None, ("rep", "fast"), None),
        P(None, ("rep", "fast"), None),
        P(None, ("rep", "fast"), None),
        P(None, None, "fast"),
        P("fast", None),
        P(None, None, "fast"),
        P("fast", None),
    )
    return jax.shard_map(
        local, mesh=mesh, in_specs=placed, out_specs=P(None, ("rep", "fast"), None), check_vma=False
    )
```

```python
import functools
import math

import jax
import jax.numpy as jnp
from jax import lax
from jax.experimental import pallas as pl
from jax.experimental.pallas import tpu as pltpu
from jax.sharding import PartitionSpec as P

EXPERTS = 8
TOPK = 3
STEPS = 2
CAP = 2
VMEM_GRANT = 8 * 2**20
DOWN_PIECES = 7
UP_ROWS = 7 * 256


def slot_tables(step_tokens, step_ids, step_gates):
    tok_count = step_ids.shape[0]
    flat_ids = step_ids.reshape(tok_count * TOPK)
    expert_hit = (flat_ids[:, None] == jnp.arange(EXPERTS, dtype=jnp.int32)[None, :]).astype(
        jnp.int32
    )
    slot_rank = jnp.sum((jnp.cumsum(expert_hit, axis=0) - expert_hit) * expert_hit, axis=1)
    slot_index = flat_ids * CAP + slot_rank
    placed = (slot_index[:, None] == jnp.arange(EXPERTS * CAP, dtype=jnp.int32)[None, :]).astype(
        jnp.float32
    )
    selector = jnp.sum(placed.reshape(tok_count, TOPK, EXPERTS * CAP), axis=1)
    blocks = jnp.einsum(
        "ts,td->sd", selector.astype(jnp.bfloat16), step_tokens, preferred_element_type=jnp.float32
    ).astype(jnp.bfloat16)
    share_row = jnp.broadcast_to(
        (jnp.arange(TOPK) == 0).astype(jnp.float32)[None, :], (tok_count, TOPK)
    ).reshape(-1)
    gate_row = step_gates.astype(jnp.float32).reshape(-1)
    slot_coefs = jnp.einsum(
        "rs,rc->sc",
        placed,
        jnp.stack([gate_row, share_row], axis=1),
        precision=lax.Precision.HIGHEST,
    ).astype(jnp.bfloat16)
    return (blocks.reshape(EXPERTS, CAP, -1), slot_coefs.reshape(EXPERTS, CAP, 2), selector)


def send_out(blocks, slot_coefs, group_size):
    spread = jnp.repeat(blocks, group_size, axis=0)
    spread_coefs = jnp.repeat(slot_coefs, group_size, axis=0)
    arrived, arrived_coefs = (
        lax.all_to_all(spread, "fast", split_axis=0, concat_axis=0, tiled=True),
        lax.all_to_all(spread_coefs, "fast", split_axis=0, concat_axis=0, tiled=True),
    )
    return (arrived, arrived_coefs)


def expert_work(arrived, arrived_coefs, weights):
    w_gate_up, w_down, shared_gate_up, shared_down = weights
    model_width = arrived.shape[-1]
    hidden_size = w_down.shape[0]
    flat_rows = arrived.reshape(-1, model_width)
    flat_coef = arrived_coefs.reshape(-1, 2).astype(jnp.float32)
    row_count = flat_rows.shape[0]
    block_rows = math.gcd(row_count, 512)
    routed_up = w_gate_up.reshape(model_width, 2 * hidden_size)
    common_up = shared_gate_up.reshape(model_width, 2 * hidden_size)

    def one_block(block_pair):
        row_block, slot_coef = block_pair
        routed = jnp.dot(row_block, routed_up, preferred_element_type=jnp.float32)
        routed_hidden = (jax.nn.silu(routed[:, :hidden_size]) * routed[:, hidden_size:]).astype(
            jnp.bfloat16
        )
        common = jnp.dot(row_block, common_up, preferred_element_type=jnp.float32)
        common_hidden = (jax.nn.silu(common[:, :hidden_size]) * common[:, hidden_size:]).astype(
            jnp.bfloat16
        )
        result = slot_coef[:, 0:1] * jnp.dot(
            routed_hidden, w_down, preferred_element_type=jnp.float32
        )
        result = result + slot_coef[:, 1:2] * jnp.dot(
            common_hidden, shared_down, preferred_element_type=jnp.float32
        )
        return result.astype(jnp.bfloat16)

    outcome = lax.map(
        one_block,
        (flat_rows.reshape(-1, block_rows, model_width), flat_coef.reshape(-1, block_rows, 2)),
    )
    return outcome.reshape(arrived.shape)


def round_trip(blocks, slot_coefs, weights, group_size):
    arrived, arrived_coefs = send_out(blocks, slot_coefs, group_size)
    partials = expert_work(arrived, arrived_coefs, weights)
    returned = lax.all_to_all(partials, "fast", split_axis=0, concat_axis=0, tiled=True)
    slot_count = blocks.shape[1]
    return returned.reshape(EXPERTS, group_size, slot_count, -1).astype(jnp.float32).sum(axis=1)


def finish(selector, summed):
    flat_sums = summed.reshape(selector.shape[1], -1)
    return jnp.dot(
        selector, flat_sums, precision=lax.Precision.HIGHEST, preferred_element_type=jnp.float32
    ).astype(jnp.bfloat16)


def local(tokens, expert_ids, gate_weights, w_gate_up, w_down, shared_gate_up, shared_down):
    group_size = lax.axis_size("fast") // EXPERTS
    if group_size == 2 and w_down.shape[0] % 256 == 0 and tokens.shape[-1] % (DOWN_PIECES * 1024) == 0:
        return by_chip(
            tokens, expert_ids, gate_weights, w_gate_up, w_down, shared_gate_up, shared_down
        )
    weights = (w_gate_up, w_down, shared_gate_up, shared_down)
    prepared = [
        slot_tables(tokens[step_index], expert_ids[step_index], gate_weights[step_index])
        for step_index in range(STEPS)
    ]
    outputs = []
    model_width = tokens.shape[-1]
    blocks = jnp.stack([member[0] for member in prepared], axis=1).reshape(
        EXPERTS, STEPS * CAP, model_width
    )
    slot_coefs = jnp.stack([member[1] for member in prepared], axis=1).reshape(
        EXPERTS, STEPS * CAP, 2
    )
    summed = round_trip(blocks, slot_coefs, weights, group_size).reshape(
        EXPERTS, STEPS, CAP, model_width
    )
    for step_index in range(STEPS):
        outputs.append(finish(prepared[step_index][2], summed[:, step_index]))
    return jnp.stack(outputs, axis=0)


def vm_params(flops=0, moved=0):
    return dict(
        compiler_params=pltpu.CompilerParams(vmem_limit_bytes=VMEM_GRANT),
        cost_estimate=pl.CostEstimate(flops=flops, bytes_accessed=moved, transcendentals=0),
    )


def in_vmem():
    return pl.BlockSpec(memory_space=pltpu.VMEM)


def in_smem():
    return pl.BlockSpec(memory_space=pltpu.SMEM)


def anywhere():
    return pl.BlockSpec(memory_space=pltpu.HBM)


def in_hbm(x):
    return pltpu.with_memory_space_constraint(x, pltpu.HBM)


def core_side():
    return lax.rem(lax.axis_index("fast"), 2)


def slot_numbers(ids_ref):
    choices, steps, tok_count = ids_ref.shape
    numbers = {}
    for s in range(steps):
        ids = [[ids_ref[k, s, t] for k in range(choices)] for t in range(tok_count)]
        for t in range(tok_count):
            for k in range(choices):
                rank = jnp.int32(0)
                for earlier in range(t):
                    for other in ids[earlier]:
                        rank = rank + (other == ids[t][k]).astype(jnp.int32)
                numbers[s, t, k] = ids[t][k] * (steps * CAP) + s * CAP + rank
    return numbers


def stacked_tokens(tok_ref):
    parts = [tok_ref[s].astype(jnp.float32) for s in range(tok_ref.shape[0])]
    return jnp.concatenate(parts, axis=0).astype(jnp.bfloat16)


def pack_kernel(ids_hbm, tok_hbm, send_ref, flat_ref, ids_ref, tok_ref, sems):
    copies = [
        pltpu.make_async_copy(ids_hbm, ids_ref, sems.at[0]),
        pltpu.make_async_copy(tok_hbm, tok_ref, sems.at[1]),
    ]
    for copy in copies:
        copy.start()
    steps, tok_count, width = tok_ref.shape
    rows, slots = steps * tok_count, EXPERTS * steps * CAP
    half = width // 2
    copies[0].wait()
    numbers = slot_numbers(ids_ref)
    place = lax.broadcasted_iota(jnp.int32, (slots, rows), 0) * rows + lax.broadcasted_iota(
        jnp.int32, (slots, rows), 1
    )
    selector = jnp.zeros((slots, rows), jnp.float32)
    for (s, t, k), number in numbers.items():
        selector = jnp.where(place == number * rows + (s * tok_count + t), 1.0, selector)
    copies[1].wait()
    flat = stacked_tokens(tok_ref)
    flat_ref[...] = flat
    blocks = jnp.dot(selector.astype(jnp.bfloat16), flat, preferred_element_type=jnp.float32)
    per = steps * CAP
    for e in range(EXPERTS):
        for g in range(2):
            piece = blocks[e * per : (e + 1) * per, g * half : (g + 1) * half]
            send_ref[2 * e + g] = piece.astype(jnp.bfloat16)


def pack_tokens(tokens, expert_ids):
    steps, tok_count, width = tokens.shape
    return pl.pallas_call(
        pack_kernel,
        out_shape=(
            jax.ShapeDtypeStruct((2 * EXPERTS, steps * CAP, width // 2), jnp.bfloat16),
            jax.ShapeDtypeStruct((steps * tok_count, width), jnp.bfloat16),
        ),
        in_specs=[anywhere(), anywhere()],
        out_specs=(in_vmem(), in_vmem()),
        scratch_shapes=[
            pltpu.SMEM(expert_ids.shape, jnp.int32),
            pltpu.VMEM(tokens.shape, jnp.bfloat16),
            pltpu.SemaphoreType.DMA((2,)),
        ],
        name="pack_tokens",
        **vm_params(10**6, 10**6),
    )(expert_ids, tokens)


def up_copies(up_ref, held_ref, sems, first):
    depth = held_ref.shape[1]
    return [
        pltpu.make_async_copy(
            up_ref.at[pl.ds(first, depth), :, pl.ds(c * 128, 128)], held_ref.at[c], sems.at[c]
        )
        for c in range(held_ref.shape[0])
    ]


def rows_in_turn(held):
    return held.reshape(held.shape[0], -1, 128)


def spread_matrix():
    row = lax.broadcasted_iota(jnp.int32, (128, 512), 0)
    col = lax.broadcasted_iota(jnp.int32, (128, 512), 1)
    target = jnp.where(col < 256, 2 * row, 2 * row + 257)
    return jnp.where(col == target, 1.0, 0.0).astype(jnp.bfloat16)


def spread_rows(x_ref, spread_ref):
    rows, width = x_ref.shape
    batch = math.gcd(width // 128, 14)
    matrix = spread_matrix()

    def step(i, carry):
        at = pl.multiple_of(i * 128 * batch, 128 * batch)
        chunk = jnp.concatenate(
            [x_ref[:, pl.ds(at + 128 * b, 128)] for b in range(batch)], axis=0
        )
        wide = jnp.dot(chunk, matrix, preferred_element_type=jnp.float32).astype(jnp.bfloat16)
        to = pl.multiple_of(i * 256 * batch, 256 * batch)
        for b in range(batch):
            piece = wide[b * rows : (b + 1) * rows]
            spread_ref[0:rows, pl.ds(to + 256 * b, 256)] = piece[:, :256]
            spread_ref[rows : 2 * rows, pl.ds(to + 256 * b, 256)] = piece[:, 256:]
        return carry

    lax.fori_loop(0, width // (128 * batch), step, 0)


def up_matmul(spread_ref, up_ref, acc_ref):
    depth = spread_ref.shape[1]
    chunk = math.gcd(depth, UP_ROWS)

    def step(i, carry):
        src = pl.ds(pl.multiple_of(i * chunk, chunk), chunk)
        rows = spread_ref[:, src]
        for p in range(up_ref.shape[0] // 2):
            pair = jnp.concatenate([up_ref[2 * p, src, :], up_ref[2 * p + 1, src, :]], axis=1)
            acc_ref[:, p * 256 : (p + 1) * 256] += jnp.dot(
                rows, pair, preferred_element_type=jnp.float32
            )
        return carry

    lax.fori_loop(0, depth // chunk, step, 0)


def hidden_of(acc_ref):
    rows = acc_ref.shape[0] // 2
    gate, up = acc_ref[0:rows], acc_ref[rows : 2 * rows]
    return (jax.nn.silu(gate) * up).astype(jnp.bfloat16)


def flatten_rows(block_ref, flat_ref):
    sources, per, _ = block_ref.shape
    group = max(1, 16 // per)
    for i in range(0, sources, group):
        rows = jnp.concatenate(
            [block_ref[i + j].astype(jnp.float32) for j in range(group)], axis=0
        )
        flat_ref[i * per : (i + group) * per] = rows.astype(flat_ref.dtype)


def half_fetch_kernel(block_ref, up_ref, held_ref, spread_ref, sems, flat_ref):
    copies = up_copies(up_ref, held_ref, sems, core_side() * held_ref.shape[1])
    for copy in copies:
        copy.start()
    flatten_rows(block_ref, flat_ref)
    spread_rows(flat_ref, spread_ref)
    for copy in copies:
        copy.wait()


def first_up_kernel(ready_ref, spread_ref, block_ref, up_ref, held_ref, next_ref, acc_ref, sems,
                    flat_ref):
    copies = up_copies(up_ref, held_ref, sems, (1 - core_side()) * held_ref.shape[1])
    for copy in copies:
        copy.start()
    flatten_rows(block_ref, flat_ref)
    spread_rows(flat_ref, next_ref)
    acc_ref[...] = jnp.zeros_like(acc_ref)
    up_matmul(spread_ref, ready_ref, acc_ref)
    for copy in copies:
        copy.wait()


def second_up_kernel(ready_ref, spread_ref, part_ref, down_ref, hid_ref, held_ref, out_ref, sems,
                     acc_ref):
    half = out_ref.shape[1]
    chunk = half // 2
    side = core_side()

    def piece(first, i):
        at = pl.ds(pl.multiple_of(first + i * chunk, chunk), chunk)
        return pltpu.make_async_copy(down_ref.at[:, at], held_ref.at[:, at], sems.at[i])

    theirs = [piece((1 - side) * half, i) for i in range(2)]
    mine = pl.ds(pl.multiple_of(side * half, half), half)
    rest = pltpu.make_async_copy(
        down_ref.at[:, mine], held_ref.at[:, mine], sems.at[2]
    )
    for copy in theirs:
        copy.start()
    rest.start()
    acc_ref[...] = part_ref[...]
    up_matmul(spread_ref, ready_ref, acc_ref)
    hid_ref[...] = hidden_of(acc_ref)
    for i, copy in enumerate(theirs):
        copy.wait()
        at = pl.ds(pl.multiple_of((1 - side) * half + i * chunk, chunk), chunk)
        out_ref[:, i * chunk : (i + 1) * chunk] = jnp.dot(
            hid_ref[...], held_ref[:, at], preferred_element_type=jnp.float32
        ).astype(out_ref.dtype)
    rest.wait()


def own_down_kernel(hid_ref, down_ref, out_ref):
    half = out_ref.shape[1]
    first = core_side() * half
    for at in (0, half // 2):
        out_ref[:, at : at + half // 2] = jnp.dot(
            hid_ref[...],
            down_ref[:, pl.ds(pl.multiple_of(first + at, 256), half // 2)],
            preferred_element_type=jnp.float32,
        )


def routed_part(mine, up, down, swap):
    sources, per, half = mine.shape
    rows, hidden = sources * per, down.shape[0]
    tiles = hidden // 128
    held_half = pltpu.VMEM((tiles, half, 2, 128), jnp.bfloat16)
    spread = pltpu.VMEM((2 * rows, 2 * half), jnp.bfloat16)
    sems = pltpu.SemaphoreType.DMA((tiles,))
    flat = pltpu.VMEM((rows, half), jnp.bfloat16)
    theirs = swap(mine)
    held, spread_mine = pl.pallas_call(
        half_fetch_kernel,
        out_shape=(held_half, spread),
        in_specs=[in_vmem(), anywhere()],
        out_specs=(in_vmem(), in_vmem()),
        scratch_shapes=[sems, flat],
        name="half_fetch",
        **vm_params(0, up.size),
    )(mine, up)
    held, spread_theirs, part = pl.pallas_call(
        first_up_kernel,
        out_shape=(
            held_half, spread, pltpu.VMEM((2 * rows, hidden), jnp.float32)
        ),
        in_specs=[in_vmem()] * 3 + [anywhere()],
        out_specs=(in_vmem(),) * 3,
        scratch_shapes=[sems, flat],
        name="first_up",
        **vm_params(8 * rows * half * hidden, up.size),
    )(rows_in_turn(held), spread_mine, theirs, up)
    hid, down_held, sent = pl.pallas_call(
        second_up_kernel,
        out_shape=(
            pltpu.VMEM((rows, hidden), jnp.bfloat16),
            pltpu.VMEM(down.shape, jnp.bfloat16),
            jax.ShapeDtypeStruct((rows, half), jnp.bfloat16),
        ),
        in_specs=[in_vmem()] * 3 + [anywhere()],
        out_specs=(in_vmem(),) * 3,
        scratch_shapes=[
            pltpu.SemaphoreType.DMA((3,)),
            pltpu.VMEM((2 * rows, hidden), jnp.float32),
        ],
        name="second_up",
        **vm_params(10 * rows * half * hidden, 2 * down.size),
    )(rows_in_turn(held), spread_theirs, part, down)
    got = swap(sent)
    kept = pl.pallas_call(
        own_down_kernel,
        out_shape=pltpu.VMEM((rows, half), jnp.float32),
        in_specs=[in_vmem()] * 2,
        out_specs=in_vmem(),
        name="own_down",
        **vm_params(2 * rows * half * hidden, 10**7),
    )(hid, down_held)
    return pl.pallas_call(
        add_kernel,
        out_shape=jax.ShapeDtypeStruct(mine.shape, jnp.bfloat16),
        in_specs=[in_vmem()] * 2,
        out_specs=anywhere(),
        scratch_shapes=[
            pltpu.VMEM(mine.shape, jnp.bfloat16),
            pltpu.SemaphoreType.DMA((math.gcd(sources, 4),)),
        ],
        name="add_halves",
        **vm_params(rows * half, 10**6),
    )(kept, got)


def add_kernel(kept_ref, got_ref, out_hbm, out_ref, sems):
    count, per, _ = out_ref.shape
    group = count // sems.shape[0]
    copies = []
    for i in range(sems.shape[0]):
        rows = slice(i * group * per, (i + 1) * group * per)
        total = kept_ref[rows] + got_ref[rows].astype(jnp.float32)
        for j in range(group):
            out_ref[i * group + j] = total[j * per : (j + 1) * per].astype(jnp.bfloat16)
        part = pl.ds(i * group, group)
        copies.append(pltpu.make_async_copy(out_ref.at[part], out_hbm.at[part], sems.at[i]))
        copies[-1].start()
    for copy in copies:
        copy.wait()


def join_rows(mine_ref, theirs_ref, first, flat_ref):
    rows, depth = flat_ref.shape
    flat_ref[0 : rows // 2] = mine_ref[:, first : first + depth]
    flat_ref[rows // 2 : rows] = theirs_ref[:, first : first + depth]


def shared_fetch_kernel(mine_ref, theirs_ref, up_ref, held_ref, spread_ref, sems, flat_ref):
    copies = up_copies(up_ref, held_ref, sems, 0)
    for copy in copies:
        copy.start()
    join_rows(mine_ref, theirs_ref, 0, flat_ref)
    spread_rows(flat_ref, spread_ref)
    for copy in copies:
        copy.wait()


def shared_first_kernel(ready_ref, spread_ref, mine_ref, theirs_ref, up_ref, held_ref, next_ref,
                        last_ref, acc_ref, sems, flat_ref, end_ref):
    depth = held_ref.shape[1]
    copies = up_copies(up_ref, held_ref, sems, depth)
    for copy in copies:
        copy.start()
    join_rows(mine_ref, theirs_ref, depth, flat_ref)
    spread_rows(flat_ref, next_ref)
    join_rows(mine_ref, theirs_ref, 2 * depth, end_ref)
    spread_rows(end_ref, last_ref)
    acc_ref[...] = jnp.zeros_like(acc_ref)
    up_matmul(spread_ref, ready_ref, acc_ref)
    for copy in copies:
        copy.wait()


def shared_second_kernel(ready_ref, spread_ref, part_ref, acc_ref):
    acc_ref[...] = part_ref[...]
    up_matmul(spread_ref, ready_ref, acc_ref)


def shared_start(mine, theirs, up):
    width, _, hidden = up.shape
    rows, tiles = 2 * mine.shape[0], hidden // 128
    depth = 3 * width // 8
    held_piece = pltpu.VMEM((tiles, depth, 2, 128), jnp.bfloat16)
    spread = pltpu.VMEM((2 * rows, 2 * depth), jnp.bfloat16)
    last = jax.ShapeDtypeStruct((2 * rows, 2 * (width - 2 * depth)), jnp.bfloat16)
    sums = (2 * rows, hidden)
    sems = pltpu.SemaphoreType.DMA((tiles,))
    flat = pltpu.VMEM((rows, depth), jnp.bfloat16)
    held, spread_now = pl.pallas_call(
        shared_fetch_kernel,
        out_shape=(held_piece, spread),
        in_specs=[in_vmem(), in_vmem(), anywhere()],
        out_specs=(in_vmem(), in_vmem()),
        scratch_shapes=[sems, flat],
        name="shared_fetch",
        **vm_params(0, up.size),
    )(mine, theirs, up)
    held, spread_now, spread_last, part = pl.pallas_call(
        shared_first_kernel,
        out_shape=(held_piece, spread, last, pltpu.VMEM(sums, jnp.float32)),
        in_specs=[in_vmem()] * 4 + [anywhere()],
        out_specs=(in_vmem(),) * 4,
        scratch_shapes=[sems, flat, pltpu.VMEM((rows, width - 2 * depth), jnp.bfloat16)],
        name="shared_first",
        **vm_params(0, up.size),
    )(rows_in_turn(held), spread_now, mine, theirs, up)
    part = pl.pallas_call(
        shared_second_kernel,
        out_shape=jax.ShapeDtypeStruct(sums, jnp.float32),
        in_specs=[in_vmem()] * 3,
        out_specs=in_vmem(),
        name="shared_second",
        **vm_params(0, up.size // 2),
    )(rows_in_turn(held), spread_now, part)
    return part, spread_last


def shared_last_kernel(part_ref, up_ref, held_ref, sems):
    del part_ref
    depth = held_ref.shape[1]
    copies = up_copies(up_ref, held_ref, sems, up_ref.shape[0] - depth)
    for copy in copies:
        copy.start()
    for copy in copies:
        copy.wait()


def shared_down_kernel(ready_ref, spread_ref, part_ref, ids_ref, gates_ref, down_ref, mine_ref,
                       theirs_ref, weight_ref, acc_ref, held_ref, sems):
    count, _, chunk = held_ref.shape
    rows = mine_ref.shape[0]
    copies = [
        pltpu.make_async_copy(
            down_ref.at[:, pl.ds(i * chunk, chunk)], held_ref.at[i], sems.at[i]
        )
        for i in range(count)
    ]
    for copy in copies:
        copy.start()
    weight_ref[...] = slot_weights(ids_ref, gates_ref)
    acc_ref[...] = part_ref[...]
    up_matmul(spread_ref, ready_ref, acc_ref)
    hid = hidden_of(acc_ref)
    for i, copy in enumerate(copies):
        copy.wait()
        part = jnp.dot(hid, held_ref[i], preferred_element_type=jnp.float32)
        cols = slice(i * chunk, (i + 1) * chunk)
        mine_ref[:, cols] = part[0:rows]
        theirs_ref[:, cols] = part[rows : 2 * rows].astype(jnp.bfloat16)


def shared_finish(part, spread_last, up, down, ids, gates):
    rows, (hidden, width) = part.shape[0] // 4, down.shape
    tiles, depth, chunk = hidden // 128, spread_last.shape[1] // 2, width // (2 * DOWN_PIECES)
    _, steps, tok_count = ids.shape
    held = pl.pallas_call(
        shared_last_kernel,
        out_shape=pltpu.VMEM((tiles, depth, 2, 128), jnp.bfloat16),
        in_specs=[anywhere(), anywhere()],
        out_specs=in_vmem(),
        scratch_shapes=[pltpu.SemaphoreType.DMA((tiles,))],
        name="shared_last",
        **vm_params(0, up.size // 2),
    )(part, up)
    return pl.pallas_call(
        shared_down_kernel,
        out_shape=(
            jax.ShapeDtypeStruct((rows, width), jnp.float32),
            jax.ShapeDtypeStruct((rows, width), jnp.bfloat16),
            jax.ShapeDtypeStruct((steps * tok_count, EXPERTS * steps * CAP), jnp.bfloat16),
        ),
        in_specs=[in_vmem()] * 3 + [in_smem(), in_smem(), anywhere()],
        out_specs=(in_vmem(),) * 3,
        scratch_shapes=[
            pltpu.VMEM(part.shape, jnp.float32),
            pltpu.VMEM((2 * DOWN_PIECES, hidden, chunk), jnp.bfloat16),
            pltpu.SemaphoreType.DMA((2 * DOWN_PIECES,)),
        ],
        name="shared_down",
        compiler_params=pltpu.CompilerParams(vmem_limit_bytes=3 * VMEM_GRANT),
        cost_estimate=pl.CostEstimate(
            flops=0, bytes_accessed=2 * down.size, transcendentals=0
        ),
    )(rows_in_turn(held), spread_last, part, ids, gates, down)


def slot_weights(ids_ref, gates_ref):
    _, steps, tok_count = ids_ref.shape
    rows, slots = steps * tok_count, EXPERTS * steps * CAP
    place = lax.broadcasted_iota(jnp.int32, (rows, slots), 0) * slots + lax.broadcasted_iota(
        jnp.int32, (rows, slots), 1
    )
    weights = jnp.zeros((rows, slots), jnp.float32)
    for (s, t, k), number in slot_numbers(ids_ref).items():
        weights = jnp.where(
            place == (s * tok_count + t) * slots + number, gates_ref[k, s, t], weights
        )
    return weights.astype(jnp.bfloat16)


def combine_kernel(weight_ref, back_ref, kept_ref, got_ref, out_ref):
    steps, tok_count, width = out_ref.shape
    half = width // 2
    weights = weight_ref[...]
    for g in range(2):
        parts = jnp.concatenate(
            [back_ref[2 * e + g].astype(jnp.float32) for e in range(EXPERTS)], axis=0
        ).astype(jnp.bfloat16)
        total = jnp.dot(weights, parts, preferred_element_type=jnp.float32)
        cols = slice(g * half, (g + 1) * half)
        total = total + (kept_ref[:, cols] + got_ref[:, cols].astype(jnp.float32))
        for s in range(steps):
            out_ref[s, :, cols] = total[s * tok_count : (s + 1) * tok_count].astype(jnp.bfloat16)


def combine(weights, back, kept, got, like):
    return pl.pallas_call(
        combine_kernel,
        out_shape=jax.ShapeDtypeStruct(like.shape, jnp.bfloat16),
        in_specs=[in_vmem()] * 4,
        out_specs=in_vmem(),
        name="combine",
        **vm_params(10**6, 10**6),
    )(weights, back, kept, got)


def by_chip(tokens, expert_ids, gate_weights, w_gate_up, w_down, shared_gate_up, shared_down):
    pairs = [(i, i ^ 1) for i in range(lax.axis_size("fast"))]

    def swap(x):
        return lax.ppermute(x, "fast", pairs)

    def exchange(x):
        return lax.all_to_all(x, "fast", split_axis=0, concat_axis=0, tiled=True)

    gates = jnp.transpose(gate_weights, (2, 0, 1)).astype(jnp.float32)
    expert_ids = jnp.transpose(expert_ids, (2, 0, 1))
    weights = (w_gate_up, w_down, shared_gate_up, shared_down)
    w_gate_up, w_down, shared_gate_up, shared_down = (in_hbm(w) for w in weights)
    send, flat = pack_tokens(in_hbm(tokens), in_hbm(expert_ids))
    arrived = exchange(send)
    part, spread_last = shared_start(flat, swap(flat), shared_gate_up)
    arrived, part = lax.optimization_barrier((arrived, part))
    partials = routed_part(arrived, w_gate_up, w_down, swap)
    partials, part = lax.optimization_barrier((partials, part))
    back = exchange(partials)
    kept, sent, slots = shared_finish(
        part, spread_last, shared_gate_up, shared_down, expert_ids, gates
    )
    return combine(slots, back, kept, swap(sent), tokens)


def solution(mesh):
    placed = (
        P(None, ("rep", "fast"), None),
        P(None, ("rep", "fast"), None),
        P(None, ("rep", "fast"), None),
        P(None, None, "fast"),
        P("fast", None),
        P(None, None, "fast"),
        P("fast", None),
    )
    return jax.shard_map(
        local, mesh=mesh, in_specs=placed, out_specs=P(None, ("rep", "fast"), None), check_vma=False
    )
```

```python
import functools
import math

import jax
import jax.numpy as jnp
from jax import lax
from jax.experimental import pallas as pl
from jax.experimental.pallas import tpu as pltpu
from jax.sharding import PartitionSpec as P

EXPERTS = 8
TOPK = 3
STEPS = 2
CAP = 2
VMEM_GRANT = 8 * 2**20
DOWN_PIECES = 7
UP_ROWS = 7 * 256


def slot_tables(step_tokens, step_ids, step_gates):
    tok_count = step_ids.shape[0]
    flat_ids = step_ids.reshape(tok_count * TOPK)
    expert_hit = (flat_ids[:, None] == jnp.arange(EXPERTS, dtype=jnp.int32)[None, :]).astype(
        jnp.int32
    )
    slot_rank = jnp.sum((jnp.cumsum(expert_hit, axis=0) - expert_hit) * expert_hit, axis=1)
    slot_index = flat_ids * CAP + slot_rank
    placed = (slot_index[:, None] == jnp.arange(EXPERTS * CAP, dtype=jnp.int32)[None, :]).astype(
        jnp.float32
    )
    selector = jnp.sum(placed.reshape(tok_count, TOPK, EXPERTS * CAP), axis=1)
    blocks = jnp.einsum(
        "ts,td->sd", selector.astype(jnp.bfloat16), step_tokens, preferred_element_type=jnp.float32
    ).astype(jnp.bfloat16)
    share_row = jnp.broadcast_to(
        (jnp.arange(TOPK) == 0).astype(jnp.float32)[None, :], (tok_count, TOPK)
    ).reshape(-1)
    gate_row = step_gates.astype(jnp.float32).reshape(-1)
    slot_coefs = jnp.einsum(
        "rs,rc->sc",
        placed,
        jnp.stack([gate_row, share_row], axis=1),
        precision=lax.Precision.HIGHEST,
    ).astype(jnp.bfloat16)
    return (blocks.reshape(EXPERTS, CAP, -1), slot_coefs.reshape(EXPERTS, CAP, 2), selector)


def send_out(blocks, slot_coefs, group_size):
    spread = jnp.repeat(blocks, group_size, axis=0)
    spread_coefs = jnp.repeat(slot_coefs, group_size, axis=0)
    arrived, arrived_coefs = (
        lax.all_to_all(spread, "fast", split_axis=0, concat_axis=0, tiled=True),
        lax.all_to_all(spread_coefs, "fast", split_axis=0, concat_axis=0, tiled=True),
    )
    return (arrived, arrived_coefs)


def expert_work(arrived, arrived_coefs, weights):
    w_gate_up, w_down, shared_gate_up, shared_down = weights
    model_width = arrived.shape[-1]
    hidden_size = w_down.shape[0]
    flat_rows = arrived.reshape(-1, model_width)
    flat_coef = arrived_coefs.reshape(-1, 2).astype(jnp.float32)
    row_count = flat_rows.shape[0]
    block_rows = math.gcd(row_count, 512)
    routed_up = w_gate_up.reshape(model_width, 2 * hidden_size)
    common_up = shared_gate_up.reshape(model_width, 2 * hidden_size)

    def one_block(block_pair):
        row_block, slot_coef = block_pair
        routed = jnp.dot(row_block, routed_up, preferred_element_type=jnp.float32)
        routed_hidden = (jax.nn.silu(routed[:, :hidden_size]) * routed[:, hidden_size:]).astype(
            jnp.bfloat16
        )
        common = jnp.dot(row_block, common_up, preferred_element_type=jnp.float32)
        common_hidden = (jax.nn.silu(common[:, :hidden_size]) * common[:, hidden_size:]).astype(
            jnp.bfloat16
        )
        result = slot_coef[:, 0:1] * jnp.dot(
            routed_hidden, w_down, preferred_element_type=jnp.float32
        )
        result = result + slot_coef[:, 1:2] * jnp.dot(
            common_hidden, shared_down, preferred_element_type=jnp.float32
        )
        return result.astype(jnp.bfloat16)

    outcome = lax.map(
        one_block,
        (flat_rows.reshape(-1, block_rows, model_width), flat_coef.reshape(-1, block_rows, 2)),
    )
    return outcome.reshape(arrived.shape)


def round_trip(blocks, slot_coefs, weights, group_size):
    arrived, arrived_coefs = send_out(blocks, slot_coefs, group_size)
    partials = expert_work(arrived, arrived_coefs, weights)
    returned = lax.all_to_all(partials, "fast", split_axis=0, concat_axis=0, tiled=True)
    slot_count = blocks.shape[1]
    return returned.reshape(EXPERTS, group_size, slot_count, -1).astype(jnp.float32).sum(axis=1)


def finish(selector, summed):
    flat_sums = summed.reshape(selector.shape[1], -1)
    return jnp.dot(
        selector, flat_sums, precision=lax.Precision.HIGHEST, preferred_element_type=jnp.float32
    ).astype(jnp.bfloat16)


def local(tokens, expert_ids, gate_weights, w_gate_up, w_down, shared_gate_up, shared_down):
    group_size = lax.axis_size("fast") // EXPERTS
    if group_size == 2 and w_down.shape[0] % 256 == 0 and tokens.shape[-1] % (DOWN_PIECES * 1024) == 0:
        return by_chip(
            tokens, expert_ids, gate_weights, w_gate_up, w_down, shared_gate_up, shared_down
        )
    weights = (w_gate_up, w_down, shared_gate_up, shared_down)
    prepared = [
        slot_tables(tokens[step_index], expert_ids[step_index], gate_weights[step_index])
        for step_index in range(STEPS)
    ]
    outputs = []
    model_width = tokens.shape[-1]
    blocks = jnp.stack([member[0] for member in prepared], axis=1).reshape(
        EXPERTS, STEPS * CAP, model_width
    )
    slot_coefs = jnp.stack([member[1] for member in prepared], axis=1).reshape(
        EXPERTS, STEPS * CAP, 2
    )
    summed = round_trip(blocks, slot_coefs, weights, group_size).reshape(
        EXPERTS, STEPS, CAP, model_width
    )
    for step_index in range(STEPS):
        outputs.append(finish(prepared[step_index][2], summed[:, step_index]))
    return jnp.stack(outputs, axis=0)


def vm_params(flops=0, moved=0):
    return dict(
        compiler_params=pltpu.CompilerParams(vmem_limit_bytes=VMEM_GRANT),
        cost_estimate=pl.CostEstimate(flops=flops, bytes_accessed=moved, transcendentals=0),
    )


def in_vmem():
    return pl.BlockSpec(memory_space=pltpu.VMEM)


def in_smem():
    return pl.BlockSpec(memory_space=pltpu.SMEM)


def anywhere():
    return pl.BlockSpec(memory_space=pltpu.HBM)


def in_hbm(x):
    return pltpu.with_memory_space_constraint(x, pltpu.HBM)


def core_side():
    return lax.rem(lax.axis_index("fast"), 2)


def slot_numbers(ids_ref):
    choices, steps, tok_count = ids_ref.shape
    numbers = {}
    for s in range(steps):
        ids = [[ids_ref[k, s, t] for k in range(choices)] for t in range(tok_count)]
        for t in range(tok_count):
            for k in range(choices):
                rank = jnp.int32(0)
                for earlier in range(t):
                    for other in ids[earlier]:
                        rank = rank + (other == ids[t][k]).astype(jnp.int32)
                numbers[s, t, k] = ids[t][k] * (steps * CAP) + s * CAP + rank
    return numbers


def stacked_tokens(tok_ref):
    parts = [tok_ref[s].astype(jnp.float32) for s in range(tok_ref.shape[0])]
    return jnp.concatenate(parts, axis=0).astype(jnp.bfloat16)


def pack_kernel(ids_hbm, tok_hbm, send_ref, flat_ref, ids_ref, tok_ref, sems):
    copies = [
        pltpu.make_async_copy(ids_hbm, ids_ref, sems.at[0]),
        pltpu.make_async_copy(tok_hbm, tok_ref, sems.at[1]),
    ]
    for copy in copies:
        copy.start()
    steps, tok_count, width = tok_ref.shape
    rows, slots = steps * tok_count, EXPERTS * steps * CAP
    half = width // 2
    copies[0].wait()
    numbers = slot_numbers(ids_ref)
    place = lax.broadcasted_iota(jnp.int32, (slots, rows), 0) * rows + lax.broadcasted_iota(
        jnp.int32, (slots, rows), 1
    )
    selector = jnp.zeros((slots, rows), jnp.float32)
    for (s, t, k), number in numbers.items():
        selector = jnp.where(place == number * rows + (s * tok_count + t), 1.0, selector)
    copies[1].wait()
    flat = stacked_tokens(tok_ref)
    flat_ref[...] = flat
    blocks = jnp.dot(selector.astype(jnp.bfloat16), flat, preferred_element_type=jnp.float32)
    per = steps * CAP
    for e in range(EXPERTS):
        for g in range(2):
            piece = blocks[e * per : (e + 1) * per, g * half : (g + 1) * half]
            send_ref[2 * e + g] = piece.astype(jnp.bfloat16)


def pack_tokens(tokens, expert_ids):
    steps, tok_count, width = tokens.shape
    return pl.pallas_call(
        pack_kernel,
        out_shape=(
            jax.ShapeDtypeStruct((2 * EXPERTS, steps * CAP, width // 2), jnp.bfloat16),
            jax.ShapeDtypeStruct((steps * tok_count, width), jnp.bfloat16),
        ),
        in_specs=[anywhere(), anywhere()],
        out_specs=(in_vmem(), in_vmem()),
        scratch_shapes=[
            pltpu.SMEM(expert_ids.shape, jnp.int32),
            pltpu.VMEM(tokens.shape, jnp.bfloat16),
            pltpu.SemaphoreType.DMA((2,)),
        ],
        name="pack_tokens",
        **vm_params(10**6, 10**6),
    )(expert_ids, tokens)


def up_copies(up_ref, held_ref, sems, first):
    depth = held_ref.shape[1]
    return [
        pltpu.make_async_copy(
            up_ref.at[pl.ds(first, depth), :, pl.ds(c * 128, 128)], held_ref.at[c], sems.at[c]
        )
        for c in range(held_ref.shape[0])
    ]


def rows_in_turn(held):
    return held.reshape(held.shape[0], -1, 128)


def spread_matrix():
    row = lax.broadcasted_iota(jnp.int32, (128, 512), 0)
    col = lax.broadcasted_iota(jnp.int32, (128, 512), 1)
    target = jnp.where(col < 256, 2 * row, 2 * row + 257)
    return jnp.where(col == target, 1.0, 0.0).astype(jnp.bfloat16)


def spread_rows(x_ref, spread_ref):
    rows, width = x_ref.shape
    batch = math.gcd(width // 128, 14)
    matrix = spread_matrix()

    def step(i, carry):
        at = pl.multiple_of(i * 128 * batch, 128 * batch)
        chunk = jnp.concatenate(
            [x_ref[:, pl.ds(at + 128 * b, 128)] for b in range(batch)], axis=0
        )
        wide = jnp.dot(chunk, matrix, preferred_element_type=jnp.float32).astype(jnp.bfloat16)
        to = pl.multiple_of(i * 256 * batch, 256 * batch)
        for b in range(batch):
            piece = wide[b * rows : (b + 1) * rows]
            spread_ref[0:rows, pl.ds(to + 256 * b, 256)] = piece[:, :256]
            spread_ref[rows : 2 * rows, pl.ds(to + 256 * b, 256)] = piece[:, 256:]
        return carry

    lax.fori_loop(0, width // (128 * batch), step, 0)


def up_matmul(spread_ref, up_ref, acc_ref):
    depth = spread_ref.shape[1]
    chunk = math.gcd(depth, UP_ROWS)

    def step(i, carry):
        src = pl.ds(pl.multiple_of(i * chunk, chunk), chunk)
        rows = spread_ref[:, src]
        for p in range(up_ref.shape[0] // 2):
            pair = jnp.concatenate([up_ref[2 * p, src, :], up_ref[2 * p + 1, src, :]], axis=1)
            acc_ref[:, p * 256 : (p + 1) * 256] += jnp.dot(
                rows, pair, preferred_element_type=jnp.float32
            )
        return carry

    lax.fori_loop(0, depth // chunk, step, 0)


def hidden_of(acc_ref):
    rows = acc_ref.shape[0] // 2
    gate, up = acc_ref[0:rows], acc_ref[rows : 2 * rows]
    return (jax.nn.silu(gate) * up).astype(jnp.bfloat16)


def flatten_rows(block_ref, flat_ref):
    sources, per, _ = block_ref.shape
    group = max(1, 16 // per)
    for i in range(0, sources, group):
        rows = jnp.concatenate(
            [block_ref[i + j].astype(jnp.float32) for j in range(group)], axis=0
        )
        flat_ref[i * per : (i + group) * per] = rows.astype(flat_ref.dtype)


def half_fetch_kernel(block_ref, up_ref, held_ref, spread_ref, sems, flat_ref):
    copies = up_copies(up_ref, held_ref, sems, core_side() * held_ref.shape[1])
    for copy in copies:
        copy.start()
    flatten_rows(block_ref, flat_ref)
    spread_rows(flat_ref, spread_ref)
    for copy in copies:
        copy.wait()


def first_up_kernel(ready_ref, spread_ref, block_ref, up_ref, held_ref, next_ref, acc_ref, sems,
                    flat_ref):
    copies = up_copies(up_ref, held_ref, sems, (1 - core_side()) * held_ref.shape[1])
    for copy in copies:
        copy.start()
    flatten_rows(block_ref, flat_ref)
    spread_rows(flat_ref, next_ref)
    acc_ref[...] = jnp.zeros_like(acc_ref)
    up_matmul(spread_ref, ready_ref, acc_ref)
    for copy in copies:
        copy.wait()


def second_up_kernel(ready_ref, spread_ref, part_ref, down_ref, hid_ref, held_ref, out_ref, sems,
                     acc_ref):
    _, per, half = out_ref.shape
    chunk = half // 2
    side = core_side()

    def piece(first, i):
        at = pl.ds(pl.multiple_of(first + i * chunk, chunk), chunk)
        return pltpu.make_async_copy(down_ref.at[:, at], held_ref.at[:, at], sems.at[i])

    theirs = [piece((1 - side) * half, i) for i in range(2)]
    mine = pl.ds(pl.multiple_of(side * half, half), half)
    rest = pltpu.make_async_copy(
        down_ref.at[:, mine], held_ref.at[:, mine], sems.at[2]
    )
    for copy in theirs:
        copy.start()
    rest.start()
    acc_ref[...] = part_ref[...]
    up_matmul(spread_ref, ready_ref, acc_ref)
    hid_ref[...] = hidden_of(acc_ref)
    for i, copy in enumerate(theirs):
        copy.wait()
        at = pl.ds(pl.multiple_of((1 - side) * half + i * chunk, chunk), chunk)
        total = jnp.dot(hid_ref[...], held_ref[:, at], preferred_element_type=jnp.float32)
        for j in range(out_ref.shape[0]):
            out_ref[j, :, i * chunk : (i + 1) * chunk] = total[j * per : (j + 1) * per].astype(
                out_ref.dtype
            )
    rest.wait()


def own_down_kernel(hid_ref, down_ref, out_ref):
    half = out_ref.shape[1]
    first = core_side() * half
    for at in (0, half // 2):
        out_ref[:, at : at + half // 2] = jnp.dot(
            hid_ref[...],
            down_ref[:, pl.ds(pl.multiple_of(first + at, 256), half // 2)],
            preferred_element_type=jnp.float32,
        )


def routed_part(mine, up, down, swap):
    sources, per, half = mine.shape
    rows, hidden = sources * per, down.shape[0]
    tiles = hidden // 128
    held_half = pltpu.VMEM((tiles, half, 2, 128), jnp.bfloat16)
    spread = pltpu.VMEM((2 * rows, 2 * half), jnp.bfloat16)
    sems = pltpu.SemaphoreType.DMA((tiles,))
    flat = pltpu.VMEM((rows, half), jnp.bfloat16)
    theirs = swap(mine)
    held, spread_mine = pl.pallas_call(
        half_fetch_kernel,
        out_shape=(held_half, spread),
        in_specs=[in_vmem(), anywhere()],
        out_specs=(in_vmem(), in_vmem()),
        scratch_shapes=[sems, flat],
        name="half_fetch",
        **vm_params(0, up.size),
    )(mine, up)
    held, spread_theirs, part = pl.pallas_call(
        first_up_kernel,
        out_shape=(
            held_half, spread, pltpu.VMEM((2 * rows, hidden), jnp.float32)
        ),
        in_specs=[in_vmem()] * 3 + [anywhere()],
        out_specs=(in_vmem(),) * 3,
        scratch_shapes=[sems, flat],
        name="first_up",
        **vm_params(8 * rows * half * hidden, up.size),
    )(rows_in_turn(held), spread_mine, theirs, up)
    hid, down_held, sent = pl.pallas_call(
        second_up_kernel,
        out_shape=(
            pltpu.VMEM((rows, hidden), jnp.bfloat16),
            pltpu.VMEM(down.shape, jnp.bfloat16),
            jax.ShapeDtypeStruct(mine.shape, jnp.bfloat16),
        ),
        in_specs=[in_vmem()] * 3 + [anywhere()],
        out_specs=(in_vmem(),) * 3,
        scratch_shapes=[
            pltpu.SemaphoreType.DMA((3,)),
            pltpu.VMEM((2 * rows, hidden), jnp.float32),
        ],
        name="second_up",
        **vm_params(10 * rows * half * hidden, 2 * down.size),
    )(rows_in_turn(held), spread_theirs, part, down)
    got = swap(sent)
    kept = pl.pallas_call(
        own_down_kernel,
        out_shape=pltpu.VMEM((rows, half), jnp.float32),
        in_specs=[in_vmem()] * 2,
        out_specs=in_vmem(),
        name="own_down",
        **vm_params(2 * rows * half * hidden, 10**7),
    )(hid, down_held)
    return pl.pallas_call(
        add_kernel,
        out_shape=jax.ShapeDtypeStruct(mine.shape, jnp.bfloat16),
        in_specs=[in_vmem()] * 2,
        out_specs=anywhere(),
        scratch_shapes=[
            pltpu.VMEM(mine.shape, jnp.bfloat16),
            pltpu.SemaphoreType.DMA((math.gcd(sources, 4),)),
        ],
        name="add_halves",
        **vm_params(rows * half, 10**6),
    )(kept, got)


def add_kernel(kept_ref, got_ref, out_hbm, out_ref, sems):
    count, per, _ = out_ref.shape
    group = count // sems.shape[0]
    copies = []
    for i in range(sems.shape[0]):
        kept = kept_ref[i * group * per : (i + 1) * group * per]
        for j in range(group):
            total = kept[j * per : (j + 1) * per] + got_ref[i * group + j].astype(jnp.float32)
            out_ref[i * group + j] = total.astype(jnp.bfloat16)
        part = pl.ds(i * group, group)
        copies.append(pltpu.make_async_copy(out_ref.at[part], out_hbm.at[part], sems.at[i]))
        copies[-1].start()
    for copy in copies:
        copy.wait()


def join_rows(mine_ref, theirs_ref, first, flat_ref):
    rows, depth = flat_ref.shape
    flat_ref[0 : rows // 2] = mine_ref[:, first : first + depth]
    flat_ref[rows // 2 : rows] = theirs_ref[:, first : first + depth]


def shared_fetch_kernel(mine_ref, theirs_ref, up_ref, held_ref, spread_ref, sems, flat_ref):
    copies = up_copies(up_ref, held_ref, sems, 0)
    for copy in copies:
        copy.start()
    join_rows(mine_ref, theirs_ref, 0, flat_ref)
    spread_rows(flat_ref, spread_ref)
    for copy in copies:
        copy.wait()


def shared_first_kernel(ready_ref, spread_ref, mine_ref, theirs_ref, up_ref, held_ref, next_ref,
                        last_ref, acc_ref, sems, flat_ref, end_ref):
    depth = held_ref.shape[1]
    copies = up_copies(up_ref, held_ref, sems, depth)
    for copy in copies:
        copy.start()
    join_rows(mine_ref, theirs_ref, depth, flat_ref)
    spread_rows(flat_ref, next_ref)
    join_rows(mine_ref, theirs_ref, 2 * depth, end_ref)
    spread_rows(end_ref, last_ref)
    acc_ref[...] = jnp.zeros_like(acc_ref)
    up_matmul(spread_ref, ready_ref, acc_ref)
    for copy in copies:
        copy.wait()


def shared_second_kernel(ready_ref, spread_ref, part_ref, acc_ref):
    acc_ref[...] = part_ref[...]
    up_matmul(spread_ref, ready_ref, acc_ref)


def shared_start(mine, theirs, up):
    width, _, hidden = up.shape
    rows, tiles = 2 * mine.shape[0], hidden // 128
    depth = 3 * width // 8
    held_piece = pltpu.VMEM((tiles, depth, 2, 128), jnp.bfloat16)
    spread = pltpu.VMEM((2 * rows, 2 * depth), jnp.bfloat16)
    last = jax.ShapeDtypeStruct((2 * rows, 2 * (width - 2 * depth)), jnp.bfloat16)
    sums = (2 * rows, hidden)
    sems = pltpu.SemaphoreType.DMA((tiles,))
    flat = pltpu.VMEM((rows, depth), jnp.bfloat16)
    held, spread_now = pl.pallas_call(
        shared_fetch_kernel,
        out_shape=(held_piece, spread),
        in_specs=[in_vmem(), in_vmem(), anywhere()],
        out_specs=(in_vmem(), in_vmem()),
        scratch_shapes=[sems, flat],
        name="shared_fetch",
        **vm_params(0, up.size),
    )(mine, theirs, up)
    held, spread_now, spread_last, part = pl.pallas_call(
        shared_first_kernel,
        out_shape=(held_piece, spread, last, pltpu.VMEM(sums, jnp.float32)),
        in_specs=[in_vmem()] * 4 + [anywhere()],
        out_specs=(in_vmem(),) * 4,
        scratch_shapes=[sems, flat, pltpu.VMEM((rows, width - 2 * depth), jnp.bfloat16)],
        name="shared_first",
        **vm_params(0, up.size),
    )(rows_in_turn(held), spread_now, mine, theirs, up)
    part = pl.pallas_call(
        shared_second_kernel,
        out_shape=jax.ShapeDtypeStruct(sums, jnp.float32),
        in_specs=[in_vmem()] * 3,
        out_specs=in_vmem(),
        name="shared_second",
        **vm_params(0, up.size // 2),
    )(rows_in_turn(held), spread_now, part)
    return part, spread_last


def shared_last_kernel(part_ref, up_ref, held_ref, sems):
    del part_ref
    depth = held_ref.shape[1]
    copies = up_copies(up_ref, held_ref, sems, up_ref.shape[0] - depth)
    for copy in copies:
        copy.start()
    for copy in copies:
        copy.wait()


def shared_down_kernel(ready_ref, spread_ref, part_ref, ids_ref, gates_ref, down_ref, mine_ref,
                       theirs_ref, weight_ref, acc_ref, held_ref, sems):
    count, _, chunk = held_ref.shape
    rows = mine_ref.shape[0]
    copies = [
        pltpu.make_async_copy(
            down_ref.at[:, pl.ds(i * chunk, chunk)], held_ref.at[i], sems.at[i]
        )
        for i in range(count)
    ]
    for copy in copies:
        copy.start()
    weight_ref[...] = slot_weights(ids_ref, gates_ref)
    acc_ref[...] = part_ref[...]
    up_matmul(spread_ref, ready_ref, acc_ref)
    hid = hidden_of(acc_ref)
    for i, copy in enumerate(copies):
        copy.wait()
        part = jnp.dot(hid, held_ref[i], preferred_element_type=jnp.float32)
        cols = slice(i * chunk, (i + 1) * chunk)
        mine_ref[:, cols] = part[0:rows]
        theirs_ref[:, cols] = part[rows : 2 * rows].astype(jnp.bfloat16)


def shared_finish(part, spread_last, up, down, ids, gates):
    rows, (hidden, width) = part.shape[0] // 4, down.shape
    tiles, depth, chunk = hidden // 128, spread_last.shape[1] // 2, width // (2 * DOWN_PIECES)
    _, steps, tok_count = ids.shape
    held = pl.pallas_call(
        shared_last_kernel,
        out_shape=pltpu.VMEM((tiles, depth, 2, 128), jnp.bfloat16),
        in_specs=[anywhere(), anywhere()],
        out_specs=in_vmem(),
        scratch_shapes=[pltpu.SemaphoreType.DMA((tiles,))],
        name="shared_last",
        **vm_params(0, up.size // 2),
    )(part, up)
    return pl.pallas_call(
        shared_down_kernel,
        out_shape=(
            jax.ShapeDtypeStruct((rows, width), jnp.float32),
            jax.ShapeDtypeStruct((rows, width), jnp.bfloat16),
            jax.ShapeDtypeStruct((steps * tok_count, EXPERTS * steps * CAP), jnp.bfloat16),
        ),
        in_specs=[in_vmem()] * 3 + [in_smem(), in_smem(), anywhere()],
        out_specs=(in_vmem(),) * 3,
        scratch_shapes=[
            pltpu.VMEM(part.shape, jnp.float32),
            pltpu.VMEM((2 * DOWN_PIECES, hidden, chunk), jnp.bfloat16),
            pltpu.SemaphoreType.DMA((2 * DOWN_PIECES,)),
        ],
        name="shared_down",
        compiler_params=pltpu.CompilerParams(vmem_limit_bytes=3 * VMEM_GRANT),
        cost_estimate=pl.CostEstimate(
            flops=0, bytes_accessed=2 * down.size, transcendentals=0
        ),
    )(rows_in_turn(held), spread_last, part, ids, gates, down)


def slot_weights(ids_ref, gates_ref):
    _, steps, tok_count = ids_ref.shape
    rows, slots = steps * tok_count, EXPERTS * steps * CAP
    place = lax.broadcasted_iota(jnp.int32, (rows, slots), 0) * slots + lax.broadcasted_iota(
        jnp.int32, (rows, slots), 1
    )
    weights = jnp.zeros((rows, slots), jnp.float32)
    for (s, t, k), number in slot_numbers(ids_ref).items():
        weights = jnp.where(
            place == (s * tok_count + t) * slots + number, gates_ref[k, s, t], weights
        )
    return weights.astype(jnp.bfloat16)


def combine_kernel(weight_ref, back_ref, kept_ref, got_ref, out_ref):
    steps, tok_count, width = out_ref.shape
    half = width // 2
    weights = weight_ref[...]
    for g in range(2):
        parts = jnp.concatenate(
            [back_ref[2 * e + g].astype(jnp.float32) for e in range(EXPERTS)], axis=0
        ).astype(jnp.bfloat16)
        total = jnp.dot(weights, parts, preferred_element_type=jnp.float32)
        cols = slice(g * half, (g + 1) * half)
        total = total + (kept_ref[:, cols] + got_ref[:, cols].astype(jnp.float32))
        for s in range(steps):
            out_ref[s, :, cols] = total[s * tok_count : (s + 1) * tok_count].astype(jnp.bfloat16)


def combine(weights, back, kept, got, like):
    return pl.pallas_call(
        combine_kernel,
        out_shape=jax.ShapeDtypeStruct(like.shape, jnp.bfloat16),
        in_specs=[in_vmem()] * 4,
        out_specs=in_vmem(),
        name="combine",
        **vm_params(10**6, 10**6),
    )(weights, back, kept, got)


def by_chip(tokens, expert_ids, gate_weights, w_gate_up, w_down, shared_gate_up, shared_down):
    pairs = [(i, i ^ 1) for i in range(lax.axis_size("fast"))]

    def swap(x):
        return lax.ppermute(x, "fast", pairs)

    def exchange(x):
        return lax.all_to_all(x, "fast", split_axis=0, concat_axis=0, tiled=True)

    gates = jnp.transpose(gate_weights, (2, 0, 1)).astype(jnp.float32)
    expert_ids = jnp.transpose(expert_ids, (2, 0, 1))
    weights = (w_gate_up, w_down, shared_gate_up, shared_down)
    w_gate_up, w_down, shared_gate_up, shared_down = (in_hbm(w) for w in weights)
    send, flat = pack_tokens(in_hbm(tokens), in_hbm(expert_ids))
    arrived = exchange(send)
    part, spread_last = shared_start(flat, swap(flat), shared_gate_up)
    arrived, part = lax.optimization_barrier((arrived, part))
    partials = routed_part(arrived, w_gate_up, w_down, swap)
    partials, part = lax.optimization_barrier((partials, part))
    back = exchange(partials)
    kept, sent, slots = shared_finish(
        part, spread_last, shared_gate_up, shared_down, expert_ids, gates
    )
    return combine(slots, back, kept, swap(sent), tokens)


def solution(mesh):
    placed = (
        P(None, ("rep", "fast"), None),
        P(None, ("rep", "fast"), None),
        P(None, ("rep", "fast"), None),
        P(None, None, "fast"),
        P("fast", None),
        P(None, None, "fast"),
        P("fast", None),
    )
    return jax.shard_map(
        local, mesh=mesh, in_specs=placed, out_specs=P(None, ("rep", "fast"), None), check_vma=False
    )
```

```python
import functools
import math

import jax
import jax.numpy as jnp
from jax import lax
from jax.experimental import pallas as pl
from jax.experimental.pallas import tpu as pltpu
from jax.sharding import PartitionSpec as P

EXPERTS = 8
TOPK = 3
STEPS = 2
CAP = 2
VMEM_GRANT = 8 * 2**20
DOWN_PIECES = 7
UP_ROWS = 7 * 256


def slot_tables(step_tokens, step_ids, step_gates):
    tok_count = step_ids.shape[0]
    flat_ids = step_ids.reshape(tok_count * TOPK)
    expert_hit = (flat_ids[:, None] == jnp.arange(EXPERTS, dtype=jnp.int32)[None, :]).astype(
        jnp.int32
    )
    slot_rank = jnp.sum((jnp.cumsum(expert_hit, axis=0) - expert_hit) * expert_hit, axis=1)
    slot_index = flat_ids * CAP + slot_rank
    placed = (slot_index[:, None] == jnp.arange(EXPERTS * CAP, dtype=jnp.int32)[None, :]).astype(
        jnp.float32
    )
    selector = jnp.sum(placed.reshape(tok_count, TOPK, EXPERTS * CAP), axis=1)
    blocks = jnp.einsum(
        "ts,td->sd", selector.astype(jnp.bfloat16), step_tokens, preferred_element_type=jnp.float32
    ).astype(jnp.bfloat16)
    share_row = jnp.broadcast_to(
        (jnp.arange(TOPK) == 0).astype(jnp.float32)[None, :], (tok_count, TOPK)
    ).reshape(-1)
    gate_row = step_gates.astype(jnp.float32).reshape(-1)
    slot_coefs = jnp.einsum(
        "rs,rc->sc",
        placed,
        jnp.stack([gate_row, share_row], axis=1),
        precision=lax.Precision.HIGHEST,
    ).astype(jnp.bfloat16)
    return (blocks.reshape(EXPERTS, CAP, -1), slot_coefs.reshape(EXPERTS, CAP, 2), selector)


def send_out(blocks, slot_coefs, group_size):
    spread = jnp.repeat(blocks, group_size, axis=0)
    spread_coefs = jnp.repeat(slot_coefs, group_size, axis=0)
    arrived, arrived_coefs = (
        lax.all_to_all(spread, "fast", split_axis=0, concat_axis=0, tiled=True),
        lax.all_to_all(spread_coefs, "fast", split_axis=0, concat_axis=0, tiled=True),
    )
    return (arrived, arrived_coefs)


def expert_work(arrived, arrived_coefs, weights):
    w_gate_up, w_down, shared_gate_up, shared_down = weights
    model_width = arrived.shape[-1]
    hidden_size = w_down.shape[0]
    flat_rows = arrived.reshape(-1, model_width)
    flat_coef = arrived_coefs.reshape(-1, 2).astype(jnp.float32)
    row_count = flat_rows.shape[0]
    block_rows = math.gcd(row_count, 512)
    routed_up = w_gate_up.reshape(model_width, 2 * hidden_size)
    common_up = shared_gate_up.reshape(model_width, 2 * hidden_size)

    def one_block(block_pair):
        row_block, slot_coef = block_pair
        routed = jnp.dot(row_block, routed_up, preferred_element_type=jnp.float32)
        routed_hidden = (jax.nn.silu(routed[:, :hidden_size]) * routed[:, hidden_size:]).astype(
            jnp.bfloat16
        )
        common = jnp.dot(row_block, common_up, preferred_element_type=jnp.float32)
        common_hidden = (jax.nn.silu(common[:, :hidden_size]) * common[:, hidden_size:]).astype(
            jnp.bfloat16
        )
        result = slot_coef[:, 0:1] * jnp.dot(
            routed_hidden, w_down, preferred_element_type=jnp.float32
        )
        result = result + slot_coef[:, 1:2] * jnp.dot(
            common_hidden, shared_down, preferred_element_type=jnp.float32
        )
        return result.astype(jnp.bfloat16)

    outcome = lax.map(
        one_block,
        (flat_rows.reshape(-1, block_rows, model_width), flat_coef.reshape(-1, block_rows, 2)),
    )
    return outcome.reshape(arrived.shape)


def round_trip(blocks, slot_coefs, weights, group_size):
    arrived, arrived_coefs = send_out(blocks, slot_coefs, group_size)
    partials = expert_work(arrived, arrived_coefs, weights)
    returned = lax.all_to_all(partials, "fast", split_axis=0, concat_axis=0, tiled=True)
    slot_count = blocks.shape[1]
    return returned.reshape(EXPERTS, group_size, slot_count, -1).astype(jnp.float32).sum(axis=1)


def finish(selector, summed):
    flat_sums = summed.reshape(selector.shape[1], -1)
    return jnp.dot(
        selector, flat_sums, precision=lax.Precision.HIGHEST, preferred_element_type=jnp.float32
    ).astype(jnp.bfloat16)


def local(tokens, expert_ids, gate_weights, w_gate_up, w_down, shared_gate_up, shared_down):
    group_size = lax.axis_size("fast") // EXPERTS
    if group_size == 2 and w_down.shape[0] % 256 == 0 and tokens.shape[-1] % (DOWN_PIECES * 1024) == 0:
        return by_chip(
            tokens, expert_ids, gate_weights, w_gate_up, w_down, shared_gate_up, shared_down
        )
    weights = (w_gate_up, w_down, shared_gate_up, shared_down)
    prepared = [
        slot_tables(tokens[step_index], expert_ids[step_index], gate_weights[step_index])
        for step_index in range(STEPS)
    ]
    outputs = []
    model_width = tokens.shape[-1]
    blocks = jnp.stack([member[0] for member in prepared], axis=1).reshape(
        EXPERTS, STEPS * CAP, model_width
    )
    slot_coefs = jnp.stack([member[1] for member in prepared], axis=1).reshape(
        EXPERTS, STEPS * CAP, 2
    )
    summed = round_trip(blocks, slot_coefs, weights, group_size).reshape(
        EXPERTS, STEPS, CAP, model_width
    )
    for step_index in range(STEPS):
        outputs.append(finish(prepared[step_index][2], summed[:, step_index]))
    return jnp.stack(outputs, axis=0)


def vm_params(flops=0, moved=0):
    return dict(
        compiler_params=pltpu.CompilerParams(vmem_limit_bytes=VMEM_GRANT),
        cost_estimate=pl.CostEstimate(flops=flops, bytes_accessed=moved, transcendentals=0),
    )


def in_vmem():
    return pl.BlockSpec(memory_space=pltpu.VMEM)


def in_smem():
    return pl.BlockSpec(memory_space=pltpu.SMEM)


def anywhere():
    return pl.BlockSpec(memory_space=pltpu.HBM)


def in_hbm(x):
    return pltpu.with_memory_space_constraint(x, pltpu.HBM)


def core_side():
    return lax.rem(lax.axis_index("fast"), 2)


def slot_numbers(ids_ref):
    choices, steps, tok_count = ids_ref.shape
    numbers = {}
    for s in range(steps):
        ids = [[ids_ref[k, s, t] for k in range(choices)] for t in range(tok_count)]
        for t in range(tok_count):
            for k in range(choices):
                rank = jnp.int32(0)
                for earlier in range(t):
                    for other in ids[earlier]:
                        rank = rank + (other == ids[t][k]).astype(jnp.int32)
                numbers[s, t, k] = ids[t][k] * (steps * CAP) + s * CAP + rank
    return numbers


def stacked_tokens(tok_ref):
    parts = [tok_ref[s].astype(jnp.float32) for s in range(tok_ref.shape[0])]
    return jnp.concatenate(parts, axis=0).astype(jnp.bfloat16)


def pack_kernel(ids_hbm, tok_hbm, send_ref, flat_ref, ids_ref, tok_ref, sems):
    copies = [
        pltpu.make_async_copy(ids_hbm, ids_ref, sems.at[0]),
        pltpu.make_async_copy(tok_hbm, tok_ref, sems.at[1]),
    ]
    for copy in copies:
        copy.start()
    steps, tok_count, width = tok_ref.shape
    rows, slots = steps * tok_count, EXPERTS * steps * CAP
    half = width // 2
    copies[0].wait()
    numbers = slot_numbers(ids_ref)
    place = lax.broadcasted_iota(jnp.int32, (slots, rows), 0) * rows + lax.broadcasted_iota(
        jnp.int32, (slots, rows), 1
    )
    selector = jnp.zeros((slots, rows), jnp.float32)
    for (s, t, k), number in numbers.items():
        selector = jnp.where(place == number * rows + (s * tok_count + t), 1.0, selector)
    copies[1].wait()
    flat = stacked_tokens(tok_ref)
    flat_ref[...] = flat
    blocks = jnp.dot(selector.astype(jnp.bfloat16), flat, preferred_element_type=jnp.float32)
    per = steps * CAP
    for e in range(EXPERTS):
        for g in range(2):
            piece = blocks[e * per : (e + 1) * per, g * half : (g + 1) * half]
            send_ref[2 * e + g] = piece.astype(jnp.bfloat16)


def pack_tokens(tokens, expert_ids):
    steps, tok_count, width = tokens.shape
    return pl.pallas_call(
        pack_kernel,
        out_shape=(
            jax.ShapeDtypeStruct((2 * EXPERTS, steps * CAP, width // 2), jnp.bfloat16),
            jax.ShapeDtypeStruct((steps * tok_count, width), jnp.bfloat16),
        ),
        in_specs=[anywhere(), anywhere()],
        out_specs=(in_vmem(), in_vmem()),
        scratch_shapes=[
            pltpu.SMEM(expert_ids.shape, jnp.int32),
            pltpu.VMEM(tokens.shape, jnp.bfloat16),
            pltpu.SemaphoreType.DMA((2,)),
        ],
        name="pack_tokens",
        **vm_params(10**6, 10**6),
    )(expert_ids, tokens)


def up_copies(up_ref, held_ref, sems, first):
    depth = held_ref.shape[1]
    return [
        pltpu.make_async_copy(
            up_ref.at[pl.ds(first, depth), :, pl.ds(c * 128, 128)], held_ref.at[c], sems.at[c]
        )
        for c in range(held_ref.shape[0])
    ]


def rows_in_turn(held):
    return held.reshape(held.shape[0], -1, 128)


def spread_matrix():
    row = lax.broadcasted_iota(jnp.int32, (128, 512), 0)
    col = lax.broadcasted_iota(jnp.int32, (128, 512), 1)
    target = jnp.where(col < 256, 2 * row, 2 * row + 257)
    return jnp.where(col == target, 1.0, 0.0).astype(jnp.bfloat16)


def spread_rows(x_ref, spread_ref):
    rows, width = x_ref.shape
    batch = math.gcd(width // 128, 14)
    matrix = spread_matrix()

    def step(i, carry):
        at = pl.multiple_of(i * 128 * batch, 128 * batch)
        chunk = jnp.concatenate(
            [x_ref[:, pl.ds(at + 128 * b, 128)] for b in range(batch)], axis=0
        )
        wide = jnp.dot(chunk, matrix, preferred_element_type=jnp.float32).astype(jnp.bfloat16)
        to = pl.multiple_of(i * 256 * batch, 256 * batch)
        for b in range(batch):
            piece = wide[b * rows : (b + 1) * rows]
            spread_ref[0:rows, pl.ds(to + 256 * b, 256)] = piece[:, :256]
            spread_ref[rows : 2 * rows, pl.ds(to + 256 * b, 256)] = piece[:, 256:]
        return carry

    lax.fori_loop(0, width // (128 * batch), step, 0)


def up_matmul(spread_ref, up_ref, acc_ref):
    depth = spread_ref.shape[1]
    chunk = math.gcd(depth, UP_ROWS)

    def step(i, carry):
        src = pl.ds(pl.multiple_of(i * chunk, chunk), chunk)
        rows = spread_ref[:, src]
        for p in range(up_ref.shape[0] // 2):
            pair = jnp.concatenate([up_ref[2 * p, src, :], up_ref[2 * p + 1, src, :]], axis=1)
            acc_ref[:, p * 256 : (p + 1) * 256] += jnp.dot(
                rows, pair, preferred_element_type=jnp.float32
            )
        return carry

    lax.fori_loop(0, depth // chunk, step, 0)


def hidden_of(acc_ref):
    rows = acc_ref.shape[0] // 2
    gate, up = acc_ref[0:rows], acc_ref[rows : 2 * rows]
    return (jax.nn.silu(gate) * up).astype(jnp.bfloat16)


def flatten_rows(block_ref, flat_ref):
    sources, per, _ = block_ref.shape
    group = max(1, 16 // per)
    for i in range(0, sources, group):
        rows = jnp.concatenate(
            [block_ref[i + j].astype(jnp.float32) for j in range(group)], axis=0
        )
        flat_ref[i * per : (i + group) * per] = rows.astype(flat_ref.dtype)


def half_fetch_kernel(block_ref, up_ref, held_ref, spread_ref, sems, flat_ref):
    copies = up_copies(up_ref, held_ref, sems, core_side() * held_ref.shape[1])
    for copy in copies:
        copy.start()
    flatten_rows(block_ref, flat_ref)
    spread_rows(flat_ref, spread_ref)
    for copy in copies:
        copy.wait()


def first_up_kernel(ready_ref, spread_ref, block_ref, up_ref, held_ref, next_ref, acc_ref, sems,
                    flat_ref):
    copies = up_copies(up_ref, held_ref, sems, (1 - core_side()) * held_ref.shape[1])
    for copy in copies:
        copy.start()
    flatten_rows(block_ref, flat_ref)
    spread_rows(flat_ref, next_ref)
    acc_ref[...] = jnp.zeros_like(acc_ref)
    up_matmul(spread_ref, ready_ref, acc_ref)
    for copy in copies:
        copy.wait()


def second_up_kernel(ready_ref, spread_ref, part_ref, down_ref, hid_ref, held_ref, out_ref, sems,
                     acc_ref):
    half = out_ref.shape[1]
    chunk = half // 2
    side = core_side()

    def piece(first, i):
        at = pl.ds(pl.multiple_of(first + i * chunk, chunk), chunk)
        return pltpu.make_async_copy(down_ref.at[:, at], held_ref.at[:, at], sems.at[i])

    theirs = [piece((1 - side) * half, i) for i in range(2)]
    mine = pl.ds(pl.multiple_of(side * half, half), half)
    rest = pltpu.make_async_copy(
        down_ref.at[:, mine], held_ref.at[:, mine], sems.at[2]
    )
    for copy in theirs:
        copy.start()
    rest.start()
    acc_ref[...] = part_ref[...]
    up_matmul(spread_ref, ready_ref, acc_ref)
    hid_ref[...] = hidden_of(acc_ref)
    for i, copy in enumerate(theirs):
        copy.wait()
        at = pl.ds(pl.multiple_of((1 - side) * half + i * chunk, chunk), chunk)
        out_ref[:, i * chunk : (i + 1) * chunk] = jnp.dot(
            hid_ref[...], held_ref[:, at], preferred_element_type=jnp.float32
        ).astype(out_ref.dtype)
    rest.wait()


def own_down_kernel(hid_ref, down_ref, out_ref):
    half = out_ref.shape[1]
    first = core_side() * half
    for at in (0, half // 2):
        out_ref[:, at : at + half // 2] = jnp.dot(
            hid_ref[...],
            down_ref[:, pl.ds(pl.multiple_of(first + at, 256), half // 2)],
            preferred_element_type=jnp.float32,
        )


def routed_part(mine, up, down, swap):
    sources, per, half = mine.shape
    rows, hidden = sources * per, down.shape[0]
    tiles = hidden // 128
    held_half = pltpu.VMEM((tiles, half, 2, 128), jnp.bfloat16)
    spread = pltpu.VMEM((2 * rows, 2 * half), jnp.bfloat16)
    sems = pltpu.SemaphoreType.DMA((tiles,))
    flat = pltpu.VMEM((rows, half), jnp.bfloat16)
    theirs = swap(mine)
    held, spread_mine = pl.pallas_call(
        half_fetch_kernel,
        out_shape=(held_half, spread),
        in_specs=[in_vmem(), anywhere()],
        out_specs=(in_vmem(), in_vmem()),
        scratch_shapes=[sems, flat],
        name="half_fetch",
        **vm_params(0, up.size),
    )(mine, up)
    held, spread_theirs, part = pl.pallas_call(
        first_up_kernel,
        out_shape=(
            held_half, spread, pltpu.VMEM((2 * rows, hidden), jnp.float32)
        ),
        in_specs=[in_vmem()] * 3 + [anywhere()],
        out_specs=(in_vmem(),) * 3,
        scratch_shapes=[sems, flat],
        name="first_up",
        **vm_params(8 * rows * half * hidden, up.size),
    )(rows_in_turn(held), spread_mine, theirs, up)
    hid, down_held, sent = pl.pallas_call(
        second_up_kernel,
        out_shape=(
            pltpu.VMEM((rows, hidden), jnp.bfloat16),
            pltpu.VMEM(down.shape, jnp.bfloat16),
            jax.ShapeDtypeStruct((rows, half), jnp.bfloat16),
        ),
        in_specs=[in_vmem()] * 3 + [anywhere()],
        out_specs=(in_vmem(),) * 3,
        scratch_shapes=[
            pltpu.SemaphoreType.DMA((3,)),
            pltpu.VMEM((2 * rows, hidden), jnp.float32),
        ],
        name="second_up",
        **vm_params(10 * rows * half * hidden, 2 * down.size),
    )(rows_in_turn(held), spread_theirs, part, down)
    got = swap(sent)
    kept = pl.pallas_call(
        own_down_kernel,
        out_shape=pltpu.VMEM((rows, half), jnp.float32),
        in_specs=[in_vmem()] * 2,
        out_specs=in_vmem(),
        name="own_down",
        **vm_params(2 * rows * half * hidden, 10**7),
    )(hid, down_held)
    return pl.pallas_call(
        add_kernel,
        out_shape=jax.ShapeDtypeStruct(mine.shape, jnp.bfloat16),
        in_specs=[in_vmem()] * 2,
        out_specs=anywhere(),
        scratch_shapes=[
            pltpu.VMEM(mine.shape, jnp.bfloat16),
            pltpu.SemaphoreType.DMA((math.gcd(sources, 2),)),
        ],
        name="add_halves",
        **vm_params(rows * half, 10**6),
    )(kept, got)


def add_kernel(kept_ref, got_ref, out_hbm, out_ref, sems):
    count, per, _ = out_ref.shape
    group = count // sems.shape[0]
    copies = []
    for i in range(sems.shape[0]):
        rows = slice(i * group * per, (i + 1) * group * per)
        total = kept_ref[rows] + got_ref[rows].astype(jnp.float32)
        for j in range(group):
            out_ref[i * group + j] = total[j * per : (j + 1) * per].astype(jnp.bfloat16)
        part = pl.ds(i * group, group)
        copies.append(pltpu.make_async_copy(out_ref.at[part], out_hbm.at[part], sems.at[i]))
        copies[-1].start()
    for copy in copies:
        copy.wait()


def join_rows(mine_ref, theirs_ref, first, flat_ref):
    rows, depth = flat_ref.shape
    flat_ref[0 : rows // 2] = mine_ref[:, first : first + depth]
    flat_ref[rows // 2 : rows] = theirs_ref[:, first : first + depth]


def shared_fetch_kernel(mine_ref, theirs_ref, up_ref, held_ref, spread_ref, sems, flat_ref):
    copies = up_copies(up_ref, held_ref, sems, 0)
    for copy in copies:
        copy.start()
    join_rows(mine_ref, theirs_ref, 0, flat_ref)
    spread_rows(flat_ref, spread_ref)
    for copy in copies:
        copy.wait()


def shared_first_kernel(ready_ref, spread_ref, mine_ref, theirs_ref, up_ref, held_ref, next_ref,
                        last_ref, acc_ref, sems, flat_ref, end_ref):
    depth = held_ref.shape[1]
    copies = up_copies(up_ref, held_ref, sems, depth)
    for copy in copies:
        copy.start()
    join_rows(mine_ref, theirs_ref, depth, flat_ref)
    spread_rows(flat_ref, next_ref)
    join_rows(mine_ref, theirs_ref, 2 * depth, end_ref)
    spread_rows(end_ref, last_ref)
    acc_ref[...] = jnp.zeros_like(acc_ref)
    up_matmul(spread_ref, ready_ref, acc_ref)
    for copy in copies:
        copy.wait()


def shared_second_kernel(ready_ref, spread_ref, part_ref, acc_ref):
    acc_ref[...] = part_ref[...]
    up_matmul(spread_ref, ready_ref, acc_ref)


def shared_start(mine, theirs, up):
    width, _, hidden = up.shape
    rows, tiles = 2 * mine.shape[0], hidden // 128
    depth = 3 * width // 8
    held_piece = pltpu.VMEM((tiles, depth, 2, 128), jnp.bfloat16)
    spread = pltpu.VMEM((2 * rows, 2 * depth), jnp.bfloat16)
    last = jax.ShapeDtypeStruct((2 * rows, 2 * (width - 2 * depth)), jnp.bfloat16)
    sums = (2 * rows, hidden)
    sems = pltpu.SemaphoreType.DMA((tiles,))
    flat = pltpu.VMEM((rows, depth), jnp.bfloat16)
    held, spread_now = pl.pallas_call(
        shared_fetch_kernel,
        out_shape=(held_piece, spread),
        in_specs=[in_vmem(), in_vmem(), anywhere()],
        out_specs=(in_vmem(), in_vmem()),
        scratch_shapes=[sems, flat],
        name="shared_fetch",
        **vm_params(0, up.size),
    )(mine, theirs, up)
    held, spread_now, spread_last, part = pl.pallas_call(
        shared_first_kernel,
        out_shape=(held_piece, spread, last, pltpu.VMEM(sums, jnp.float32)),
        in_specs=[in_vmem()] * 4 + [anywhere()],
        out_specs=(in_vmem(),) * 4,
        scratch_shapes=[sems, flat, pltpu.VMEM((rows, width - 2 * depth), jnp.bfloat16)],
        name="shared_first",
        **vm_params(0, up.size),
    )(rows_in_turn(held), spread_now, mine, theirs, up)
    part = pl.pallas_call(
        shared_second_kernel,
        out_shape=jax.ShapeDtypeStruct(sums, jnp.float32),
        in_specs=[in_vmem()] * 3,
        out_specs=in_vmem(),
        name="shared_second",
        **vm_params(0, up.size // 2),
    )(rows_in_turn(held), spread_now, part)
    return part, spread_last


def shared_last_kernel(part_ref, up_ref, held_ref, sems):
    del part_ref
    depth = held_ref.shape[1]
    copies = up_copies(up_ref, held_ref, sems, up_ref.shape[0] - depth)
    for copy in copies:
        copy.start()
    for copy in copies:
        copy.wait()


def shared_down_kernel(ready_ref, spread_ref, part_ref, ids_ref, gates_ref, down_ref, mine_ref,
                       theirs_ref, weight_ref, acc_ref, held_ref, sems):
    count, _, chunk = held_ref.shape
    rows = mine_ref.shape[0]
    copies = [
        pltpu.make_async_copy(
            down_ref.at[:, pl.ds(i * chunk, chunk)], held_ref.at[i], sems.at[i]
        )
        for i in range(count)
    ]
    for copy in copies:
        copy.start()
    weight_ref[...] = slot_weights(ids_ref, gates_ref)
    acc_ref[...] = part_ref[...]
    up_matmul(spread_ref, ready_ref, acc_ref)
    hid = hidden_of(acc_ref)
    for i, copy in enumerate(copies):
        copy.wait()
        part = jnp.dot(hid, held_ref[i], preferred_element_type=jnp.float32)
        cols = slice(i * chunk, (i + 1) * chunk)
        mine_ref[:, cols] = part[0:rows]
        theirs_ref[:, cols] = part[rows : 2 * rows].astype(jnp.bfloat16)


def shared_finish(part, spread_last, up, down, ids, gates):
    rows, (hidden, width) = part.shape[0] // 4, down.shape
    tiles, depth, chunk = hidden // 128, spread_last.shape[1] // 2, width // (2 * DOWN_PIECES)
    _, steps, tok_count = ids.shape
    held = pl.pallas_call(
        shared_last_kernel,
        out_shape=pltpu.VMEM((tiles, depth, 2, 128), jnp.bfloat16),
        in_specs=[anywhere(), anywhere()],
        out_specs=in_vmem(),
        scratch_shapes=[pltpu.SemaphoreType.DMA((tiles,))],
        name="shared_last",
        **vm_params(0, up.size // 2),
    )(part, up)
    return pl.pallas_call(
        shared_down_kernel,
        out_shape=(
            jax.ShapeDtypeStruct((rows, width), jnp.float32),
            jax.ShapeDtypeStruct((rows, width), jnp.bfloat16),
            jax.ShapeDtypeStruct((steps * tok_count, EXPERTS * steps * CAP), jnp.bfloat16),
        ),
        in_specs=[in_vmem()] * 3 + [in_smem(), in_smem(), anywhere()],
        out_specs=(in_vmem(),) * 3,
        scratch_shapes=[
            pltpu.VMEM(part.shape, jnp.float32),
            pltpu.VMEM((2 * DOWN_PIECES, hidden, chunk), jnp.bfloat16),
            pltpu.SemaphoreType.DMA((2 * DOWN_PIECES,)),
        ],
        name="shared_down",
        compiler_params=pltpu.CompilerParams(vmem_limit_bytes=3 * VMEM_GRANT),
        cost_estimate=pl.CostEstimate(
            flops=0, bytes_accessed=2 * down.size, transcendentals=0
        ),
    )(rows_in_turn(held), spread_last, part, ids, gates, down)


def slot_weights(ids_ref, gates_ref):
    _, steps, tok_count = ids_ref.shape
    rows, slots = steps * tok_count, EXPERTS * steps * CAP
    place = lax.broadcasted_iota(jnp.int32, (rows, slots), 0) * slots + lax.broadcasted_iota(
        jnp.int32, (rows, slots), 1
    )
    weights = jnp.zeros((rows, slots), jnp.float32)
    for (s, t, k), number in slot_numbers(ids_ref).items():
        weights = jnp.where(
            place == (s * tok_count + t) * slots + number, gates_ref[k, s, t], weights
        )
    return weights.astype(jnp.bfloat16)


def combine_kernel(weight_ref, back_ref, kept_ref, got_ref, out_ref):
    steps, tok_count, width = out_ref.shape
    half = width // 2
    weights = weight_ref[...]
    for g in range(2):
        parts = jnp.concatenate(
            [back_ref[2 * e + g].astype(jnp.float32) for e in range(EXPERTS)], axis=0
        ).astype(jnp.bfloat16)
        total = jnp.dot(weights, parts, preferred_element_type=jnp.float32)
        cols = slice(g * half, (g + 1) * half)
        total = total + (kept_ref[:, cols] + got_ref[:, cols].astype(jnp.float32))
        for s in range(steps):
            out_ref[s, :, cols] = total[s * tok_count : (s + 1) * tok_count].astype(jnp.bfloat16)


def combine(weights, back, kept, got, like):
    return pl.pallas_call(
        combine_kernel,
        out_shape=jax.ShapeDtypeStruct(like.shape, jnp.bfloat16),
        in_specs=[in_vmem()] * 4,
        out_specs=in_vmem(),
        name="combine",
        **vm_params(10**6, 10**6),
    )(weights, back, kept, got)


def by_chip(tokens, expert_ids, gate_weights, w_gate_up, w_down, shared_gate_up, shared_down):
    pairs = [(i, i ^ 1) for i in range(lax.axis_size("fast"))]

    def swap(x):
        return lax.ppermute(x, "fast", pairs)

    def exchange(x):
        return lax.all_to_all(x, "fast", split_axis=0, concat_axis=0, tiled=True)

    gates = jnp.transpose(gate_weights, (2, 0, 1)).astype(jnp.float32)
    expert_ids = jnp.transpose(expert_ids, (2, 0, 1))
    weights = (w_gate_up, w_down, shared_gate_up, shared_down)
    w_gate_up, w_down, shared_gate_up, shared_down = (in_hbm(w) for w in weights)
    send, flat = pack_tokens(in_hbm(tokens), in_hbm(expert_ids))
    arrived = exchange(send)
    part, spread_last = shared_start(flat, swap(flat), shared_gate_up)
    arrived, part = lax.optimization_barrier((arrived, part))
    partials = routed_part(arrived, w_gate_up, w_down, swap)
    partials, part = lax.optimization_barrier((partials, part))
    back = exchange(partials)
    kept, sent, slots = shared_finish(
        part, spread_last, shared_gate_up, shared_down, expert_ids, gates
    )
    return combine(slots, back, kept, swap(sent), tokens)


def solution(mesh):
    placed = (
        P(None, ("rep", "fast"), None),
        P(None, ("rep", "fast"), None),
        P(None, ("rep", "fast"), None),
        P(None, None, "fast"),
        P("fast", None),
        P(None, None, "fast"),
        P("fast", None),
    )
    return jax.shard_map(
        local, mesh=mesh, in_specs=placed, out_specs=P(None, ("rep", "fast"), None), check_vma=False
    )
```
